256 devices in a mesh: dp: 4 (over y), expert: 64 (over x, z, core).
Axes of the slice: x: 4, y: 4, z: 8, core: 2. Of those that a mesh axis runs over, the one named last changes fastest.
Arguments:
- tokens: bfloat16 [6144, 4096], P(('dp', 'expert')), may hold values from -6 to 6
- route_ids: int32 [6144, 8], P(('dp', 'expert')), may hold values from 0 to 127, as said below
- route_weights: float32 [6144, 8], P(('dp', 'expert')), may hold values from 0.05 to 1
- placement: int32 [128], replicated, may hold values from 0 to 127, each once
- gate_up: bfloat16 [128, 4096, 1536], P('expert', None, 'dp'), may hold values from -0.09375 to 0.09375
- down: bfloat16 [128, 768, 4096], P('expert', None, 'dp'), may hold values from -0.21875 to 0.21875
- queries: bfloat16 [1024, 4, 8192], P(('dp', 'expert')), may hold values from -12 to 12
- draft_keys: bfloat16 [1024, 4, 512], P(('dp', 'expert')), may hold values from -4 to 4
- draft_values: bfloat16 [1024, 4, 512], P(('dp', 'expert')), may hold values from -6 to 6
- cache_keys: bfloat16 [1024, 256, 512], P(('dp', 'expert')), may hold values from -4 to 4
- cache_values: bfloat16 [1024, 256, 512], P(('dp', 'expert')), may hold values from -6 to 6
- cache_lengths: int32 [1024], P(('dp', 'expert')), may hold values from 1 to 256, 131072 in all
Outputs:
- mixed: bfloat16 [6144, 4096], P(('dp', 'expert'))
- context: bfloat16 [1024, 4, 8192], P(('dp', 'expert'))
The draws below stay inside these ranges and needn't reach their ends.
Inputs may be any that keep to these rules, and one draw needn't show every extreme that they name: `route_ids`: each row names 8 different experts. 2 experts, the same for the whole step, are each named by exactly 4 of the rows of every device; every other expert by 1 or 2 rows of each device, and one of them by 2 rows of every device. `placement`: each slot holds one expert; slot s lies on index s // 2 of expert. `cache_lengths`: the lengths of all requests sum to 131072.
All inputs are finite; a program needn't handle non-finite values. No bound on the sum of `cache_lengths` on one device may be relied on, other than what follows from the above.
Results may differ from the reference program's by a relative error of at most 0.0057.
Values may be sent and summed in bfloat16 or wider, within the bound.
No kernel may reach another device: no remote copies, remote signals or barrier semaphores. Data moves between devices by JAX's collectives and lax.ppermute only.
A program may use at most 128 MiB of HBM per device.

```python
import math
import jax
import jax.numpy as jnp
import numpy as np
from jax import lax

D = 4096
FF = 768
Q_HEADS = 64
KV_HEADS = 4
HEAD_DIM = 128
TOP = 8
HOT = 2
DRAFT = 4
TOK_DEV = 24
REQ_DEV = 4
CTX = 256
EXPERTS = 128
TOKENS = 6144
REQS = 1024
HOT_ROWS = 4
N_DP = 4


def draw_queries(key, part):
    full_shape = (REQS, DRAFT, KV_HEADS, Q_HEADS // KV_HEADS, HEAD_DIM)
    key = jax.random.fold_in(key, 7)
    values = jax.random.truncated_normal(key, -4.0, 4.0, full_shape, jnp.float32)
    return values.reshape(REQS, DRAFT, Q_HEADS * HEAD_DIM).astype(jnp.bfloat16)


def draw_draft_keys(key, part):
    full_shape = (REQS, DRAFT, KV_HEADS, HEAD_DIM)
    key = jax.random.fold_in(key, 9)
    values = jax.random.truncated_normal(key, -4.0, 4.0, full_shape, jnp.float32)
    return values.reshape(REQS, DRAFT, KV_HEADS * HEAD_DIM).astype(jnp.bfloat16)


def draw_route_ids(key, part):
    key = jax.random.fold_in(key, 3)
    global_key, block_key = jax.random.split(key)
    shuffled = jax.random.permutation(global_key, EXPERTS).astype(jnp.int32)
    hot_ids = shuffled[:HOT]
    cycle_base = shuffled[HOT:]
    others = EXPERTS - HOT
    blocks = TOKENS // TOK_DEV

    def one_block(this_key):
        named_key, cycle_key, column_key = jax.random.split(this_key, 3)
        named_list = []
        for hot_index in range(HOT):
            chosen_rows = jax.random.permutation(jax.random.fold_in(named_key, hot_index), TOK_DEV)[:HOT_ROWS]
            named_list.append(jnp.zeros((TOK_DEV,), jnp.int32).at[chosen_rows].set(1))
        named_table = jnp.stack(named_list)
        hot_here = jnp.sum(named_table, axis=0)
        drawn_here = TOP - hot_here
        offsets = jnp.cumsum(drawn_here) - drawn_here
        cycle_list = jnp.concatenate([cycle_base[:1], jax.random.permutation(cycle_key, cycle_base[1:])])
        columns = jnp.arange(TOP, dtype=jnp.int32)[None, :]
        hot_order = jnp.cumsum(named_table, axis=0) - named_table
        hot_value = jnp.sum(named_table[:, :, None] * (hot_order[:, :, None] == columns[None]).astype(jnp.int32) * hot_ids[:, None, None], axis=0)
        drawn_value = cycle_list[(offsets[:, None] + columns - hot_here[:, None]) % others]
        entries = jnp.where(columns < hot_here[:, None], hot_value, drawn_value)
        shuffle_scores = jax.random.randint(column_key, (TOK_DEV, TOP), 0, 1 << 20) * TOP + columns
        ordering = jnp.argsort(shuffle_scores, axis=1)
        return jnp.take_along_axis(entries, ordering, axis=1)
    routes = jax.vmap(one_block)(jax.random.split(block_key, blocks))
    return routes.reshape(TOKENS, TOP).astype(jnp.int32)


def shard_levels(key, dims, cuts, low, top_value):
    def one(dim, shards_of):
        heights = jax.random.uniform(jax.random.fold_in(jax.random.fold_in(key, 6), dim), (shards_of,), jnp.float32, low / len(cuts), top_value / len(cuts))
        return jnp.repeat(jnp.exp(heights), dims[dim] // shards_of).reshape((-1,) + (1,) * (len(dims) - dim - 1))

    gain = one(*cuts[0])
    for cut in cuts[1:]:
        gain = gain * one(*cut)
    return gain


def profile(count, total, bound, lean):
    loads = [(1 << 20) // math.isqrt(grade ** lean) + 1 for grade in range(2, count + 1)]
    surplus, given = total - bound - (count - 1), [1] * (count - 1)
    while surplus > 0:
        candidates = [i for i in range(count - 1) if given[i] < bound]
        whole, remaining = sum([loads[i] for i in candidates]), surplus
        for i in candidates:
            extra = min(bound - given[i], max(1, remaining * loads[i] // whole), surplus)
            given[i] = given[i] + extra
            surplus = surplus - extra
    return np.array([bound] + given)


def ragged(own_key, number_of, total, most, lean):
    if number_of == 2:
        one = jax.random.randint(own_key, (), max(1, total - most), min(most, total - 1) + 1)
        return jnp.stack([one, total - one])
    tallies = jnp.asarray(profile(number_of, total, most, lean), jnp.int32)
    couples = (number_of - 1) // 2
    donor, sink = tallies[1:1 + 2 * couples:2], tallies[2:2 + 2 * couples:2]
    room = jnp.minimum(donor - 1, most - sink)
    passed = jax.random.randint(jax.random.fold_in(own_key, 1), (couples,), 0, 1 << 20) % (room + 1)
    tallies = tallies.at[1:1 + 2 * couples:2].set(donor - passed).at[2:2 + 2 * couples:2].set(sink + passed)
    return tallies[jax.random.permutation(jax.random.fold_in(own_key, 2), number_of)]


def bell_draw(key, dims, scale, limit, pieces=(), held_as=jnp.bfloat16):
    loudness = shard_levels(key, dims, pieces, -0.22, 0.18) if pieces else 1.0
    drawn = jax.random.normal(key, dims, jnp.float32) * scale * loudness
    return jnp.minimum(jnp.maximum(drawn, -limit), limit).astype(held_as)


def setup_inputs(seed: int = 0) -> dict:
    streams_of = jax.random.split(jax.random.key(seed), 13)
    return {
        "tokens": bell_draw(streams_of[0], (TOKENS, D), 1.0, 6.0, ((0, 256),)),
        "route_ids": draw_route_ids(jax.random.fold_in(streams_of[12], 71), 0),
        "route_weights": jnp.clip(jnp.exp(math.log(1.0) - 2.9957323 * jax.random.uniform(streams_of[2], (TOKENS, TOP), jnp.float32) ** shard_levels(streams_of[2], (TOKENS, TOP), ((0, 256),), -0.2, 0.2)), 0.05, 1.0),
        "placement": jax.random.permutation(streams_of[3], EXPERTS).astype(jnp.int32),
        "gate_up": bell_draw(streams_of[4], (EXPERTS, D, 2 * FF), D ** -0.5, 0.09375, ((0, 64), (2, 4))),
        "down": bell_draw(streams_of[5], (EXPERTS, FF, D), FF ** -0.5, 0.21875, ((0, 64), (2, 4))),
        "queries": draw_queries(jax.random.fold_in(streams_of[12], 71), 0),
        "draft_keys": draw_draft_keys(jax.random.fold_in(streams_of[12], 71), 0),
        "draft_values": bell_draw(streams_of[8], (REQS, DRAFT, KV_HEADS * HEAD_DIM), 1.0, 6.0, ((0, 256),)),
        "cache_keys": bell_draw(streams_of[9], (REQS, CTX, KV_HEADS * HEAD_DIM), 1.0, 4.0, ((0, 256),)),
        "cache_values": bell_draw(streams_of[10], (REQS, CTX, KV_HEADS * HEAD_DIM), 1.0, 6.0, ((0, 256),)),
        "cache_lengths": ragged(streams_of[11], REQS, REQS * CTX // 2, CTX, 2).astype(jnp.int32),
    }


def attend_block(queries, draft_keys, draft_values, cache_keys, cache_values, cache_lengths):
    req_here, drafts, query_width = queries.shape
    context_len = cache_keys.shape[1]
    groups = draft_keys.shape[2] // HEAD_DIM
    per_group = query_width // (groups * HEAD_DIM)
    scaling = 1.0 / math.sqrt(HEAD_DIM)
    query_heads = queries.astype(jnp.float32).reshape(req_here, drafts, groups, per_group, HEAD_DIM)
    cache_k = cache_keys.astype(jnp.float32).reshape(req_here, context_len, groups, HEAD_DIM)
    cache_v = cache_values.astype(jnp.float32).reshape(req_here, context_len, groups, HEAD_DIM)
    draft_k = draft_keys.astype(jnp.float32).reshape(req_here, drafts, groups, HEAD_DIM)
    draft_v = draft_values.astype(jnp.float32).reshape(req_here, drafts, groups, HEAD_DIM)
    score_cache = jnp.einsum('rigpe,rcge->rgpic', query_heads, cache_k) * scaling
    score_draft = jnp.einsum('rigpe,rjge->rgpij', query_heads, draft_k) * scaling
    live_cache = jnp.arange(context_len, dtype=jnp.int32)[None, :] < cache_lengths[:, None]
    live_draft = jnp.arange(drafts, dtype=jnp.int32)[None, :] <= jnp.arange(drafts, dtype=jnp.int32)[:, None]
    score_cache = jnp.where(live_cache[:, None, None, None, :], score_cache, -1e+30)
    score_draft = jnp.where(live_draft[None, None, None, :, :], score_draft, -1e+30)
    highest = jnp.maximum(lax.optimization_barrier(jnp.max(score_cache, axis=-1)), lax.optimization_barrier(jnp.max(score_draft, axis=-1)))
    expo_cache = jnp.exp(score_cache - highest[..., None])
    expo_draft = jnp.exp(score_draft - highest[..., None])
    totals = lax.optimization_barrier(jnp.sum(expo_cache, axis=-1)) + lax.optimization_barrier(jnp.sum(expo_draft, axis=-1))
    prob_cache = (expo_cache / totals[..., None]).astype(jnp.bfloat16).astype(jnp.float32)
    prob_draft = (expo_draft / totals[..., None]).astype(jnp.bfloat16).astype(jnp.float32)
    result = jnp.einsum('rgpic,rcge->rigpe', prob_cache, cache_v) + jnp.einsum('rgpij,rjge->rigpe', prob_draft, draft_v)
    return result.astype(jnp.bfloat16).reshape(req_here, drafts, query_width)

def reference(tokens, route_ids, route_weights, placement, gate_up, down, queries, draft_keys, draft_values, cache_keys, cache_values, cache_lengths):
    flat_ids = route_ids.reshape(-1)
    ordering = jnp.argsort(flat_ids, stable=True).astype(jnp.int32)
    counts = lax.optimization_barrier(jnp.sum((flat_ids[:, None] == jnp.arange(EXPERTS, dtype=jnp.int32)[None, :]).astype(jnp.int32), axis=0))
    starts = (jnp.cumsum(counts) - counts).astype(jnp.int32)
    room = HOT_ROWS * (TOKENS // TOK_DEV)
    padded_order = jnp.concatenate([ordering, jnp.zeros((room,), jnp.int32)])
    flat_weights = route_weights.reshape(-1)
    quarter = FF // N_DP

    def one_expert(accum, expert_index):
        slot_here = placement[expert_index]
        picks = lax.dynamic_slice(padded_order, (starts[expert_index],), (room,))
        is_live = jnp.arange(room, dtype=jnp.int32) < counts[expert_index]
        tok_rows = (picks // TOP).astype(jnp.int32)
        inputs = tokens[tok_rows]
        weight_pair = gate_up[slot_here].reshape(D, N_DP, 2, quarter)
        gate = jnp.dot(inputs, weight_pair[:, :, 0, :].reshape(D, FF), preferred_element_type=jnp.float32)
        upper = jnp.dot(inputs, weight_pair[:, :, 1, :].reshape(D, FF), preferred_element_type=jnp.float32)
        hidden = (jax.nn.silu(gate) * upper).astype(jnp.bfloat16)
        expert_out = jnp.dot(hidden, down[slot_here], preferred_element_type=jnp.float32).astype(jnp.bfloat16)
        scaled = jnp.where(is_live, flat_weights[picks], 0.0)
        accum = accum.at[tok_rows].add(scaled[:, None] * expert_out.astype(jnp.float32))
        return (accum, None)
    accum, unused = lax.scan(one_expert, jnp.zeros((TOKENS, D), jnp.float32), jnp.arange(EXPERTS, dtype=jnp.int32))
    mixed = accum.astype(jnp.bfloat16)
    blocks_count = REQS // REQ_DEV

    def attend_pack(pack):
        return attend_block(pack[0], pack[1], pack[2], pack[3], pack[4], pack[5])
    packed = (queries.reshape(blocks_count, REQ_DEV, DRAFT, Q_HEADS * HEAD_DIM), draft_keys.reshape(blocks_count, REQ_DEV, DRAFT, KV_HEADS * HEAD_DIM), draft_values.reshape(blocks_count, REQ_DEV, DRAFT, KV_HEADS * HEAD_DIM), cache_keys.reshape(blocks_count, REQ_DEV, CTX, KV_HEADS * HEAD_DIM), cache_values.reshape(blocks_count, REQ_DEV, CTX, KV_HEADS * HEAD_DIM), cache_lengths.reshape(blocks_count, REQ_DEV))
    context = lax.map(attend_pack, packed).reshape(REQS, DRAFT, Q_HEADS * HEAD_DIM)
    return (mixed, context)
```

```python
import math

import jax
import jax.numpy as jnp
from jax import lax
from jax.sharding import PartitionSpec as P

HEAD_DIM = 128
HOT = 2
CAP = 2
BF = jnp.bfloat16
F32 = jnp.float32


def attend_block(queries, draft_keys, draft_values, cache_keys, cache_values, cache_lengths):
    req_here, drafts, query_width = queries.shape
    context_len = cache_keys.shape[1]
    groups = draft_keys.shape[2] // HEAD_DIM
    per_group = query_width // (groups * HEAD_DIM)
    scaling = 1.0 / math.sqrt(HEAD_DIM)
    query_heads = queries.reshape(req_here, drafts, groups, per_group, HEAD_DIM)
    cache_k = cache_keys.reshape(req_here, context_len, groups, HEAD_DIM)
    cache_v = cache_values.reshape(req_here, context_len, groups, HEAD_DIM)
    draft_k = draft_keys.reshape(req_here, drafts, groups, HEAD_DIM)
    draft_v = draft_values.reshape(req_here, drafts, groups, HEAD_DIM)
    score_cache = (
        jnp.einsum("rigpe,rcge->rgpic", query_heads, cache_k, preferred_element_type=jnp.float32)
        * scaling
    )
    score_draft = (
        jnp.einsum("rigpe,rjge->rgpij", query_heads, draft_k, preferred_element_type=jnp.float32)
        * scaling
    )
    live_cache = jnp.arange(context_len, dtype=jnp.int32)[None, :] < cache_lengths[:, None]
    live_draft = (
        jnp.arange(drafts, dtype=jnp.int32)[None, :] <= jnp.arange(drafts, dtype=jnp.int32)[:, None]
    )
    score_cache = jnp.where(live_cache[:, None, None, None, :], score_cache, -1e30)
    score_draft = jnp.where(live_draft[None, None, None, :, :], score_draft, -1e30)
    highest = jnp.maximum(jnp.max(score_cache, axis=-1), jnp.max(score_draft, axis=-1))
    expo_cache = jnp.exp(score_cache - highest[..., None])
    expo_draft = jnp.exp(score_draft - highest[..., None])
    totals = jnp.sum(expo_cache, axis=-1) + jnp.sum(expo_draft, axis=-1)
    prob_cache = (expo_cache / totals[..., None]).astype(jnp.bfloat16)
    prob_draft = (expo_draft / totals[..., None]).astype(jnp.bfloat16)
    result = jnp.einsum(
        "rgpic,rcge->rigpe", prob_cache, cache_v, preferred_element_type=jnp.float32
    )
    result = result + jnp.einsum(
        "rgpij,rjge->rigpe", prob_draft, draft_v, preferred_element_type=jnp.float32
    )
    return result.astype(jnp.bfloat16).reshape(req_here, drafts, query_width)


def shift(x, k, n):
    return lax.ppermute(x, "dp", [(i, (i + k) % n) for i in range(n)])


def dot(a, b, dims):
    return lax.dot_general(a, b, (dims, ((), ())), preferred_element_type=F32)


def split3(x):
    hi = lax.reduce_precision(x, 8, 7)
    mid = lax.reduce_precision(x - hi, 8, 7)
    lo = x - hi - mid
    return [v.astype(BF) for v in (hi, mid, lo)]


def glu(gate_up):
    half = gate_up.shape[0] // 2
    return (jax.nn.silu(gate_up[:half]) * gate_up[half:]).astype(BF)


def per_device(
    tokens,
    route_ids,
    route_weights,
    placement,
    gate_up,
    down,
    queries,
    draft_keys,
    draft_values,
    cache_keys,
    cache_values,
    cache_lengths,
):
    n_dp = lax.axis_size("dp")
    n_expert = lax.axis_size("expert")
    me = lax.axis_index("dp")
    here = lax.axis_index("expert")
    rows, picks = route_ids.shape
    slots = placement.shape[0]
    per = gate_up.shape[0]
    width = tokens.shape[1]
    part = width // n_dp
    quarter = gate_up.shape[2] // 2
    chunk = n_dp * CAP

    slot_of = jnp.sum(
        (route_ids[:, :, None] == jnp.arange(slots, dtype=jnp.int32)) * placement, axis=2
    )
    own = jnp.sum(slot_of[:, :, None] == jnp.arange(slots, dtype=jnp.int32), axis=(0, 1))
    hot = own > CAP
    slot_range = jnp.arange(slots, dtype=jnp.int32)
    hot_slots = [
        jnp.min(jnp.where(hot, slot_range, slots - 1)),
        jnp.max(jnp.where(hot, slot_range, 0)),
    ]
    hot_gate, hot_down = [], []
    for one in hot_slots:
        mine = one // per == here
        gate_one = lax.dynamic_index_in_dim(gate_up, one % per, 0, keepdims=False)
        down_one = lax.dynamic_index_in_dim(down, one % per, 0, keepdims=False)
        hot_gate.append(jnp.where(mine, gate_one, jnp.zeros_like(gate_one)))
        hot_down.append(jnp.where(mine, down_one, jnp.zeros_like(down_one)))
    hot_gate, hot_down = lax.psum((hot_gate, hot_down), "expert")

    all_tokens = lax.all_gather(tokens, "dp", axis=0, tiled=True)
    all_ids = lax.all_gather(slot_of, "dp", axis=0, tiled=True)
    all_weights = lax.all_gather(route_weights, "dp", axis=0, tiled=True)
    all_rows = n_dp * rows
    my_part = lax.dynamic_slice_in_dim(all_tokens, me * part, part, axis=1)

    gate_up_t, _ = lax.optimization_barrier((gate_up, all_tokens))
    pieces = [lax.dynamic_slice_in_dim(gate_up_t, me * part, part, axis=1)]
    for k in range(1, n_dp):
        to_send = lax.dynamic_slice_in_dim(gate_up_t, (me + k) % n_dp * part, part, axis=1)
        pieces.append(shift(to_send, k, n_dp))

    match = all_ids[:, :, None] == slot_range
    takes = jnp.any(match, axis=1)
    weight_of = jnp.sum(jnp.where(match, all_weights[:, :, None], 0.0), axis=1)
    takes_plane = takes.reshape(n_dp, rows, slots).astype(jnp.int32)
    rank = (jnp.cumsum(takes_plane, axis=1) - takes_plane).reshape(all_rows, slots)
    plane_of = jnp.arange(all_rows, dtype=jnp.int32) // rows
    code = jnp.where(takes & ~hot[None, :], plane_of[:, None] * CAP + rank, -1)
    place = code.T[:, None, :] == jnp.arange(chunk, dtype=jnp.int32)[None, :, None]
    place = place.reshape(slots * chunk, all_rows)
    combine = jnp.where(place, jnp.repeat(weight_of.T, chunk, axis=0), 0.0)

    outgoing = dot(place.astype(BF), my_part, ((1,), (0,))).astype(BF)
    arrived = lax.all_to_all(
        outgoing.reshape(n_expert, per * chunk, part), "expert", 0, 0, tiled=True
    )
    returned = []
    results = []
    for s in range(per):
        x = arrived[:, s * chunk : (s + 1) * chunk].reshape(n_expert * chunk, part)
        total = dot(pieces[0][s], x, ((0,), (1,)))
        for k in range(1, n_dp):
            partial = dot(pieces[k][s], x, ((0,), (1,))).astype(BF)
            total = total + shift(partial, n_dp - k, n_dp).astype(F32)
        hidden = glu(total)
        out = None
        for k in range(n_dp):
            piece = hidden if k == 0 else shift(hidden, k, n_dp)
            down_piece = lax.dynamic_slice_in_dim(
                down[s], (me + n_dp - k) % n_dp * quarter, quarter, axis=0
            )
            term = dot(piece, down_piece, ((0,), (0,)))
            out = term if out is None else out + term
        results.append(out.astype(BF).reshape(n_expert, chunk, part))
    back = lax.all_to_all(jnp.concatenate(results, axis=1), "expert", 0, 0, tiled=True)
    back = back.reshape(slots * chunk, part)

    mixed = sum(dot(c, back, ((0,), (0,))) for c in split3(combine))

    for h in range(HOT):
        hidden = glu(dot(hot_gate[h], all_tokens, ((0,), (1,))))
        hidden = lax.all_gather(hidden, "dp", axis=0, tiled=True)
        out = dot(hidden, hot_down[h], ((0,), (0,))).astype(BF).astype(F32)
        hot_weight = jnp.sum(jnp.where(slot_range == hot_slots[h], weight_of, 0.0), axis=1)
        mixed = mixed + hot_weight[:, None] * out

    mixed = mixed.astype(BF).reshape(n_dp, rows, part)
    mixed = lax.all_to_all(mixed, "dp", 0, 0, tiled=True)
    mixed = jnp.transpose(mixed, (1, 0, 2)).reshape(rows, width)
    context = attend_block(
        queries, draft_keys, draft_values, cache_keys, cache_values, cache_lengths
    )
    return (mixed, context)


def solution(mesh):
    in_specs = (
        P(("dp", "expert"), None),
        P(("dp", "expert"), None),
        P(("dp", "expert"), None),
        P(),
        P("expert", None, "dp"),
        P("expert", None, "dp"),
        P(("dp", "expert"), None, None),
        P(("dp", "expert"), None, None),
        P(("dp", "expert"), None, None),
        P(("dp", "expert"), None, None),
        P(("dp", "expert"), None, None),
        P(("dp", "expert")),
    )
    out_specs = (P(("dp", "expert"), None), P(("dp", "expert"), None, None))
    return jax.shard_map(
        per_device, mesh=mesh, in_specs=in_specs, out_specs=out_specs, check_vma=False
    )
```

```python
import math

import jax
import jax.numpy as jnp
from jax import lax
from jax.sharding import Mesh
from jax.sharding import PartitionSpec as P

HEAD_DIM = 128
HOT = 2
PLANE = ("x", "z", "core")
ALL = ("dp",) + PLANE
CAP = 2
BF = jnp.bfloat16
F32 = jnp.float32


def attend_block(queries, draft_keys, draft_values, cache_keys, cache_values, cache_lengths):
    req_here, drafts, query_width = queries.shape
    context_len = cache_keys.shape[1]
    groups = draft_keys.shape[2] // HEAD_DIM
    per_group = query_width // (groups * HEAD_DIM)
    scaling = 1.0 / math.sqrt(HEAD_DIM)
    query_heads = queries.reshape(req_here, drafts, groups, per_group, HEAD_DIM)
    cache_k = cache_keys.reshape(req_here, context_len, groups, HEAD_DIM)
    cache_v = cache_values.reshape(req_here, context_len, groups, HEAD_DIM)
    draft_k = draft_keys.reshape(req_here, drafts, groups, HEAD_DIM)
    draft_v = draft_values.reshape(req_here, drafts, groups, HEAD_DIM)
    score_cache = (
        jnp.einsum("rigpe,rcge->rgpic", query_heads, cache_k, preferred_element_type=jnp.float32)
        * scaling
    )
    score_draft = (
        jnp.einsum("rigpe,rjge->rgpij", query_heads, draft_k, preferred_element_type=jnp.float32)
        * scaling
    )
    live_cache = jnp.arange(context_len, dtype=jnp.int32)[None, :] < cache_lengths[:, None]
    live_draft = (
        jnp.arange(drafts, dtype=jnp.int32)[None, :] <= jnp.arange(drafts, dtype=jnp.int32)[:, None]
    )
    score_cache = jnp.where(live_cache[:, None, None, None, :], score_cache, -1e30)
    score_draft = jnp.where(live_draft[None, None, None, :, :], score_draft, -1e30)
    highest = jnp.maximum(jnp.max(score_cache, axis=-1), jnp.max(score_draft, axis=-1))
    expo_cache = jnp.exp(score_cache - highest[..., None])
    expo_draft = jnp.exp(score_draft - highest[..., None])
    totals = jnp.sum(expo_cache, axis=-1) + jnp.sum(expo_draft, axis=-1)
    prob_cache = (expo_cache / totals[..., None]).astype(jnp.bfloat16)
    prob_draft = (expo_draft / totals[..., None]).astype(jnp.bfloat16)
    result = jnp.einsum(
        "rgpic,rcge->rigpe", prob_cache, cache_v, preferred_element_type=jnp.float32
    )
    result = result + jnp.einsum(
        "rgpij,rjge->rigpe", prob_draft, draft_v, preferred_element_type=jnp.float32
    )
    return result.astype(jnp.bfloat16).reshape(req_here, drafts, query_width)


def shift(x, k, n=4):
    k = k % n
    return x if k == 0 else lax.ppermute(x, "dp", [(i, (i + k) % n) for i in range(n)])


def swap(x):
    return lax.ppermute(x, "core", [(0, 1), (1, 0)])


def dot(a, b, dims):
    return lax.dot_general(a, b, (dims, ((), ())), preferred_element_type=F32)


def split3(x):
    hi = lax.reduce_precision(x, 8, 7)
    mid = lax.reduce_precision(x - hi, 8, 7)
    lo = x - hi - mid
    return [v.astype(BF) for v in (hi, mid, lo)]


def glu(gate_up):
    half = gate_up.shape[0] // 2
    return (jax.nn.silu(gate_up[:half]) * gate_up[half:]).astype(BF)


def per_device(
    tokens,
    route_ids,
    route_weights,
    placement,
    gate_up,
    down,
    queries,
    draft_keys,
    draft_values,
    cache_keys,
    cache_values,
    cache_lengths,
):
    n_dp = lax.axis_size("dp")
    n_expert = lax.axis_size(PLANE)
    me = lax.axis_index("dp")
    here = lax.axis_index(PLANE)
    core = lax.axis_index("core")
    rows, picks = route_ids.shape
    slots = placement.shape[0]
    per = gate_up.shape[0]
    width = tokens.shape[1]
    part = width // n_dp
    quarter = gate_up.shape[2] // 2
    chunk = n_dp * CAP
    all_rows = n_dp * rows
    slot_range = jnp.arange(slots, dtype=jnp.int32)
    ks = range(n_dp)

    def features(x, k):
        return lax.dynamic_slice_in_dim(x, (me + k) % n_dp * part, part, axis=1)

    slot_of = jnp.sum(
        jnp.where(route_ids[:, :, None] == slot_range, placement, 0), axis=2
    )
    info = jnp.concatenate([slot_of.astype(F32), route_weights], axis=1)
    infos = jnp.concatenate([shift(info, k) for k in ks], axis=0)
    my_part = jnp.concatenate([shift(features(tokens, k), k) for k in ks], axis=0)

    own = jnp.sum(slot_of[:, :, None] == slot_range, axis=(0, 1))
    hot = own > CAP
    first_hot = jnp.min(jnp.where(hot, slot_range, slots - 1))
    last_hot = jnp.max(jnp.where(hot, slot_range, 0))
    my_hot = jnp.where(core == 0, first_hot, last_hot)
    other_hot = jnp.where(core == 0, last_hot, first_hot)
    sibling = here + 1 - 2 * core

    def hot_weights(weights):
        theirs = swap(lax.dynamic_index_in_dim(weights, other_hot % per, 0, keepdims=False))
        mine = lax.dynamic_index_in_dim(weights, my_hot % per, 0, keepdims=False)
        owner = my_hot // per
        return jnp.where(owner == here, mine, jnp.where(owner == sibling, theirs, 0.0))

    hot_gate, hot_down = lax.psum((hot_weights(gate_up), hot_weights(down)), ("x", "z"))

    pieces = [shift(features(gate_up, k), k) for k in ks]

    match = infos[:, :picks].astype(jnp.int32)[:, :, None] == slot_range
    takes = jnp.any(match, axis=1)
    weight_of = jnp.sum(jnp.where(match, infos[:, picks:, None], 0.0), axis=1)
    takes_plane = takes.reshape(n_dp, rows, slots).astype(jnp.int32)
    rank = (jnp.cumsum(takes_plane, axis=1) - takes_plane).reshape(all_rows, slots)
    plane_of = (me + n_dp - jnp.arange(all_rows, dtype=jnp.int32) // rows) % n_dp
    code = jnp.where(takes & ~hot[None, :], plane_of[:, None] * CAP + rank, -1)
    place = code.T[:, None, :] == jnp.arange(chunk, dtype=jnp.int32)[None, :, None]
    place = place.reshape(slots * chunk, all_rows)
    combine = jnp.where(place, jnp.repeat(weight_of.T, chunk, axis=0), 0.0)

    outgoing = dot(place.astype(BF), my_part, ((1,), (0,))).astype(BF)
    arrived = lax.all_to_all(
        outgoing.reshape(n_expert, per * chunk, part), PLANE, 0, 0, tiled=True
    )
    results = []
    for s in range(per):
        x = arrived[:, s * chunk : (s + 1) * chunk].reshape(n_expert * chunk, part)
        total = dot(pieces[0][s], x, ((0,), (1,)))
        for k in ks[1:]:
            partial = dot(pieces[k][s], x, ((0,), (1,))).astype(BF)
            total = total + shift(partial, -k).astype(F32)
        hidden = glu(total)
        out = 0.0
        for k in ks:
            down_piece = lax.dynamic_slice_in_dim(
                down[s], (me + n_dp - k) % n_dp * quarter, quarter, axis=0
            )
            out = out + dot(shift(hidden, k), down_piece, ((0,), (0,)))
        results.append(out.astype(BF).reshape(n_expert, chunk, part))
    back = lax.all_to_all(jnp.concatenate(results, axis=1), PLANE, 0, 0, tiled=True)
    back = back.reshape(slots * chunk, part)

    all_tokens = jnp.zeros((all_rows, width), BF)
    for k in ks:
        all_tokens = lax.dynamic_update_slice_in_dim(
            all_tokens, shift(tokens, k), (me + n_dp - k) % n_dp * rows, axis=0
        )
    both_tokens = jnp.concatenate([all_tokens, swap(all_tokens)], axis=0)
    hidden = glu(dot(hot_gate, both_tokens, ((0,), (1,))))
    hot_out = 0.0
    for k in ks:
        down_piece = lax.dynamic_slice_in_dim(
            hot_down, (me + n_dp - k) % n_dp * quarter, quarter, axis=0
        )
        hot_out = hot_out + dot(shift(hidden, k), down_piece, ((0,), (0,)))
    hot_out = hot_out.astype(BF)
    from_sibling = swap(hot_out[all_rows:])

    mixed = sum(dot(c, back, ((0,), (0,))) for c in split3(combine))
    for one, out in ((my_hot, hot_out[:all_rows]), (other_hot, from_sibling)):
        hot_weight = jnp.sum(jnp.where(slot_range == one, weight_of, 0.0), axis=1)
        out = jnp.concatenate(
            [lax.dynamic_slice_in_dim(out, (me + n_dp - k) % n_dp * rows, rows) for k in ks]
        )
        mixed = mixed + hot_weight[:, None] * out.astype(F32)

    mixed = mixed.astype(BF).reshape(n_dp, rows, part)
    mixed_out = jnp.zeros((rows, width), BF)
    for k in ks:
        mixed_out = lax.dynamic_update_slice_in_dim(
            mixed_out, shift(mixed[k], -k), (me + k) % n_dp * part, axis=1
        )
    context = attend_block(
        queries, draft_keys, draft_values, cache_keys, cache_values, cache_lengths
    )
    return (mixed_out, context)


def solution(mesh):
    chips = Mesh(mesh.devices.reshape(mesh.shape["dp"], 4, -1, 2), ALL)
    in_specs = (
        P(ALL, None),
        P(ALL, None),
        P(ALL, None),
        P(),
        P(PLANE, None, "dp"),
        P(PLANE, None, "dp"),
        P(ALL, None, None),
        P(ALL, None, None),
        P(ALL, None, None),
        P(ALL, None, None),
        P(ALL, None, None),
        P(ALL),
    )
    out_specs = (P(ALL, None), P(ALL, None, None))
    return jax.shard_map(
        per_device, mesh=chips, in_specs=in_specs, out_specs=out_specs, check_vma=False
    )
```

```python
import math

import jax
import jax.numpy as jnp
from jax import lax
from jax.sharding import Mesh
from jax.sharding import PartitionSpec as P

HEAD_DIM = 128
HOT = 2
CAP = 2
LANES = 128
PLANE = ("x", "z", "core")
ALL = ("dp",) + PLANE
BF = jnp.bfloat16
F32 = jnp.float32


def attend_block(queries, draft_keys, draft_values, cache_keys, cache_values, cache_lengths):
    req_here, drafts, query_width = queries.shape
    context_len = cache_keys.shape[1]
    groups = draft_keys.shape[2] // HEAD_DIM
    per_group = query_width // (groups * HEAD_DIM)
    scaling = 1.0 / math.sqrt(HEAD_DIM)
    query_heads = queries.reshape(req_here, drafts, groups, per_group, HEAD_DIM)
    cache_k = cache_keys.reshape(req_here, context_len, groups, HEAD_DIM)
    cache_v = cache_values.reshape(req_here, context_len, groups, HEAD_DIM)
    draft_k = draft_keys.reshape(req_here, drafts, groups, HEAD_DIM)
    draft_v = draft_values.reshape(req_here, drafts, groups, HEAD_DIM)
    score_cache = (
        jnp.einsum("rigpe,rcge->rgpic", query_heads, cache_k, preferred_element_type=jnp.float32)
        * scaling
    )
    score_draft = (
        jnp.einsum("rigpe,rjge->rgpij", query_heads, draft_k, preferred_element_type=jnp.float32)
        * scaling
    )
    live_cache = jnp.arange(context_len, dtype=jnp.int32)[None, :] < cache_lengths[:, None]
    live_draft = (
        jnp.arange(drafts, dtype=jnp.int32)[None, :] <= jnp.arange(drafts, dtype=jnp.int32)[:, None]
    )
    score_cache = jnp.where(live_cache[:, None, None, None, :], score_cache, -1e30)
    score_draft = jnp.where(live_draft[None, None, None, :, :], score_draft, -1e30)
    highest = jnp.maximum(jnp.max(score_cache, axis=-1), jnp.max(score_draft, axis=-1))
    expo_cache = jnp.exp(score_cache - highest[..., None])
    expo_draft = jnp.exp(score_draft - highest[..., None])
    totals = jnp.sum(expo_cache, axis=-1) + jnp.sum(expo_draft, axis=-1)
    prob_cache = (expo_cache / totals[..., None]).astype(jnp.bfloat16)
    prob_draft = (expo_draft / totals[..., None]).astype(jnp.bfloat16)
    result = jnp.einsum(
        "rgpic,rcge->rigpe", prob_cache, cache_v, preferred_element_type=jnp.float32
    )
    result = result + jnp.einsum(
        "rgpij,rjge->rigpe", prob_draft, draft_v, preferred_element_type=jnp.float32
    )
    return result.astype(jnp.bfloat16).reshape(req_here, drafts, query_width)


def ring(x, axis, k, n=4):
    k = k % n
    return x if k == 0 else lax.ppermute(x, axis, [(i, (i + k) % n) for i in range(n)])


def swap(x):
    return lax.ppermute(x, "core", [(0, 1), (1, 0)])


def after(x, *others):
    return lax.optimization_barrier((x, *others))[0]


def dot(a, b, dims, batch=()):
    return lax.dot_general(a, b, (dims, (batch, batch)), preferred_element_type=F32)


def pack(gate_one, down_one, n):
    wide = gate_one.shape[1]
    gate_one = gate_one.reshape(n, -1, wide)
    down_one = down_one.reshape(n, -1, down_one.shape[1])
    blocks = [gate_one]
    for at in range(0, down_one.shape[2], wide):
        block = down_one[:, :, at : at + wide]
        short = wide - block.shape[2]
        blocks.append(jnp.pad(block, ((0, 0), (0, 0), (0, short))) if short else block)
    return jnp.concatenate(blocks, axis=1)


def unpack(piece, gate_rows, down_rows, down_width):
    blocks = [
        piece[at : at + down_rows] for at in range(gate_rows, piece.shape[0], down_rows)
    ]
    return piece[:gate_rows], jnp.concatenate(blocks, axis=1)[:, :down_width]


def split3(x):
    hi = lax.reduce_precision(x, 8, 7)
    mid = lax.reduce_precision(x - hi, 8, 7)
    lo = x - hi - mid
    return [v.astype(BF) for v in (hi, mid, lo)]


def glu(gate_up):
    half = gate_up.shape[-2] // 2
    return (jax.nn.silu(gate_up[..., :half, :]) * gate_up[..., half:, :]).astype(BF)


def per_device(
    tokens,
    route_ids,
    route_weights,
    placement,
    gate_up,
    down,
    queries,
    draft_keys,
    draft_values,
    cache_keys,
    cache_values,
    cache_lengths,
):
    n_dp, n_x, n_z = lax.axis_size("dp"), lax.axis_size("x"), lax.axis_size("z")
    n_expert = lax.axis_size(PLANE)
    me, here = lax.axis_index("dp"), lax.axis_index(PLANE)
    here_x, here_z, core = lax.axis_index("x"), lax.axis_index("z"), lax.axis_index("core")
    rows, picks = route_ids.shape
    slots = placement.shape[0]
    per = gate_up.shape[0]
    width = tokens.shape[1]
    part = width // n_dp
    quarter = gate_up.shape[2] // 2
    chunk = n_dp * CAP
    all_rows = n_dp * rows
    slot_range = jnp.arange(slots, dtype=jnp.int32)
    ks, xs = range(n_dp), range(n_x)

    def plane(k):
        return (me + n_dp - k) % n_dp

    slot_of = jnp.sum(
        jnp.where(route_ids[:, :, None] == slot_range, placement, 0), axis=2
    )
    info = jnp.concatenate([slot_of.astype(BF)] + split3(route_weights), axis=1)
    info = jnp.pad(info, ((0, 0), (0, LANES - info.shape[1])))
    sent = jnp.concatenate([tokens, info], axis=1)
    came = [ring(sent, "dp", k) for k in ks]
    came_tokens = [x[:, :width] for x in came]
    infos = jnp.concatenate([x[:, width:] for x in came], axis=0)
    my_part = jnp.concatenate(
        [lax.dynamic_slice_in_dim(x, me * part, part, axis=1) for x in came_tokens], axis=0
    )

    own = jnp.sum(slot_of[:, :, None] == slot_range, axis=(0, 1))
    hot = own > CAP
    first_hot = jnp.min(jnp.where(hot, slot_range, slots - 1))
    last_hot = jnp.max(jnp.where(hot, slot_range, 0))
    my_hot = jnp.where(core == 0, first_hot, last_hot)
    other_hot = jnp.where(core == 0, last_hot, first_hot)

    owner = my_hot // per
    owner_x, owner_z = owner // (2 * n_z), owner // 2 % n_z

    def packed(slot):
        return pack(
            lax.dynamic_index_in_dim(gate_up, slot % per, 0, keepdims=False),
            lax.dynamic_index_in_dim(down, slot % per, 0, keepdims=False),
            n_x,
        )

    theirs = swap(packed(other_hot))
    held = jnp.where(owner == here, packed(my_hot), theirs)

    def slice_x(k):
        return lax.dynamic_index_in_dim(held, (here_x + k) % n_x, 0, keepdims=False)

    far = (here_x + n_x - owner_x) % n_x
    piece = slice_x(0)
    for k in xs[1:]:
        piece = jnp.where(far == k, ring(slice_x(k), "x", k), piece)
    piece = lax.psum(jnp.where(here_z == owner_z, piece, 0.0), "z")
    hot_pieces = [
        unpack(ring(piece, "x", k), width // n_x, down.shape[1] // n_x, part) for k in xs
    ]

    to_send = [
        lax.dynamic_slice_in_dim(gate_up, (me + k) % n_dp * part, part, axis=1) for k in ks
    ]
    pieces = [ring(x, "dp", k) for k, x in zip(ks, to_send)]

    match = infos[:, :picks].astype(jnp.int32)[:, :, None] == slot_range
    came_weights = sum(infos[:, i * picks : (i + 1) * picks].astype(F32) for i in (1, 2, 3))
    takes = jnp.any(match, axis=1)
    weight_of = jnp.sum(jnp.where(match, came_weights[:, :, None], 0.0), axis=1)
    takes_plane = takes.reshape(n_dp, rows, slots).astype(jnp.int32)
    rank = (jnp.cumsum(takes_plane, axis=1) - takes_plane).reshape(all_rows, slots)
    plane_of = (me + n_dp - jnp.arange(all_rows, dtype=jnp.int32) // rows) % n_dp
    code = jnp.where(takes & ~hot[None, :], plane_of[:, None] * CAP + rank, -1)
    place = code.T[:, None, :] == jnp.arange(chunk, dtype=jnp.int32)[None, :, None]
    place = place.reshape(slots * chunk, all_rows)
    combine = jnp.where(place, jnp.repeat(weight_of.T, chunk, axis=0), 0.0)
    combine = jnp.concatenate(split3(combine), axis=1)

    outgoing = dot(after(place.astype(BF), *to_send), my_part, ((1,), (0,))).astype(BF)
    arrived = lax.all_to_all(
        outgoing.reshape(n_expert, per * chunk, part), PLANE, 0, 0, tiled=True
    )
    x = arrived.reshape(n_expert, per, chunk, part)
    x = jnp.transpose(x, (1, 0, 2, 3)).reshape(per, n_expert * chunk, part)
    total = dot(pieces[0], x, ((1,), (2,)), (0,))
    for k in ks[1:]:
        partial = dot(pieces[k], x, ((1,), (2,)), (0,)).astype(BF)
        total = total + ring(partial, "dp", -k).astype(F32)
    hidden = glu(total)
    out = 0.0
    for k in ks:
        down_piece = lax.dynamic_slice_in_dim(down, plane(k) * quarter, quarter, axis=1)
        out = out + dot(ring(hidden, "dp", k), down_piece, ((1,), (1,)), (0,))
    out = out.astype(BF).reshape(per, n_expert, chunk, part)
    out = jnp.transpose(out, (1, 0, 2, 3)).reshape(n_expert, per * chunk, part)
    back = lax.all_to_all(out, PLANE, 0, 0, tiled=True).reshape(slots * chunk, part)

    all_tokens = jnp.zeros((all_rows, width), BF)
    for k in ks:
        all_tokens = lax.dynamic_update_slice_in_dim(
            all_tokens, came_tokens[k], plane(k) * rows, axis=0
        )
    both_tokens = jnp.concatenate([all_tokens, swap(all_tokens)], axis=0)
    gated = 0.0
    for k in xs:
        at = (here_x + n_x - k) % n_x * (width // n_x)
        some = lax.dynamic_slice_in_dim(both_tokens, at, width // n_x, axis=1)
        gated = gated + dot(hot_pieces[k][0], some, ((0,), (1,)))
    hidden_hot = glu(gated)
    hidden_all = jnp.zeros((n_dp * quarter, 2 * all_rows), BF)
    for k in ks:
        hidden_all = lax.dynamic_update_slice_in_dim(
            hidden_all, ring(hidden_hot, "dp", k), plane(k) * quarter, axis=0
        )
    hot_out = 0.0
    for k in xs:
        size = hidden_all.shape[0] // n_x
        some = lax.dynamic_slice_in_dim(hidden_all, (here_x + n_x - k) % n_x * size, size, axis=0)
        hot_out = hot_out + dot(some, hot_pieces[k][1], ((0,), (0,)))
    hot_out = hot_out.astype(BF)
    from_sibling = swap(hot_out[all_rows:])

    mixed = dot(combine, back, ((0,), (0,)))
    mixed = mixed[:all_rows] + mixed[all_rows : 2 * all_rows] + mixed[2 * all_rows :]
    for one, out in ((my_hot, hot_out[:all_rows]), (other_hot, from_sibling)):
        hot_weight = jnp.sum(jnp.where(slot_range == one, weight_of, 0.0), axis=1)
        out = jnp.concatenate(
            [lax.dynamic_slice_in_dim(out, plane(k) * rows, rows) for k in ks]
        )
        mixed = mixed + hot_weight[:, None] * out.astype(F32)

    mixed = mixed.astype(BF).reshape(n_dp, rows, part)
    mixed_out = jnp.zeros((rows, width), BF)
    for k in ks:
        mixed_out = lax.dynamic_update_slice_in_dim(
            mixed_out, ring(mixed[k], "dp", -k), (me + k) % n_dp * part, axis=1
        )
    context = attend_block(
        after(queries, hidden), draft_keys, draft_values, cache_keys, cache_values, cache_lengths
    )
    return (mixed_out, context)


def solution(mesh):
    chips = Mesh(mesh.devices.reshape(mesh.shape["dp"], 4, -1, 2), ALL)
    in_specs = (
        P(ALL, None),
        P(ALL, None),
        P(ALL, None),
        P(),
        P(PLANE, None, "dp"),
        P(PLANE, None, "dp"),
        P(ALL, None, None),
        P(ALL, None, None),
        P(ALL, None, None),
        P(ALL, None, None),
        P(ALL, None, None),
        P(ALL),
    )
    out_specs = (P(ALL, None), P(ALL, None, None))
    return jax.shard_map(
        per_device, mesh=chips, in_specs=in_specs, out_specs=out_specs, check_vma=False
    )
```

```python
import math

import jax
import jax.numpy as jnp
from jax import lax
from jax.sharding import Mesh
from jax.sharding import PartitionSpec as P

HEAD_DIM = 128
HOT = 2
CAP = 2
LANES = 128
PLANE = ("x", "z", "core")
ALL = ("dp",) + PLANE
BF = jnp.bfloat16
F32 = jnp.float32


def attend_block(queries, draft_keys, draft_values, cache_keys, cache_values, cache_lengths):
    req_here, drafts, query_width = queries.shape
    context_len = cache_keys.shape[1]
    groups = draft_keys.shape[2] // HEAD_DIM
    per_group = query_width // (groups * HEAD_DIM)
    scaling = 1.0 / math.sqrt(HEAD_DIM)
    query_heads = queries.reshape(req_here, drafts, groups, per_group, HEAD_DIM)
    cache_k = cache_keys.reshape(req_here, context_len, groups, HEAD_DIM)
    cache_v = cache_values.reshape(req_here, context_len, groups, HEAD_DIM)
    draft_k = draft_keys.reshape(req_here, drafts, groups, HEAD_DIM)
    draft_v = draft_values.reshape(req_here, drafts, groups, HEAD_DIM)
    score_cache = (
        jnp.einsum("rigpe,rcge->rgpic", query_heads, cache_k, preferred_element_type=jnp.float32)
        * scaling
    )
    score_draft = (
        jnp.einsum("rigpe,rjge->rgpij", query_heads, draft_k, preferred_element_type=jnp.float32)
        * scaling
    )
    live_cache = jnp.arange(context_len, dtype=jnp.int32)[None, :] < cache_lengths[:, None]
    live_draft = (
        jnp.arange(drafts, dtype=jnp.int32)[None, :] <= jnp.arange(drafts, dtype=jnp.int32)[:, None]
    )
    score_cache = jnp.where(live_cache[:, None, None, None, :], score_cache, -1e30)
    score_draft = jnp.where(live_draft[None, None, None, :, :], score_draft, -1e30)
    highest = jnp.maximum(jnp.max(score_cache, axis=-1), jnp.max(score_draft, axis=-1))
    expo_cache = jnp.exp(score_cache - highest[..., None])
    expo_draft = jnp.exp(score_draft - highest[..., None])
    totals = jnp.sum(expo_cache, axis=-1) + jnp.sum(expo_draft, axis=-1)
    prob_cache = (expo_cache / totals[..., None]).astype(jnp.bfloat16)
    prob_draft = (expo_draft / totals[..., None]).astype(jnp.bfloat16)
    result = jnp.einsum(
        "rgpic,rcge->rigpe", prob_cache, cache_v, preferred_element_type=jnp.float32
    )
    result = result + jnp.einsum(
        "rgpij,rjge->rigpe", prob_draft, draft_v, preferred_element_type=jnp.float32
    )
    return result.astype(jnp.bfloat16).reshape(req_here, drafts, query_width)


def ring(x, axis, k, n=4):
    k = k % n
    return x if k == 0 else lax.ppermute(x, axis, [(i, (i + k) % n) for i in range(n)])


def swap(x):
    return lax.ppermute(x, "core", [(0, 1), (1, 0)])


def after(x, *others):
    return lax.optimization_barrier((x, *others))[0]


def dot(a, b, dims, batch=()):
    return lax.dot_general(a, b, (dims, (batch, batch)), preferred_element_type=F32)


def pack(gate_one, down_one, n):
    wide = gate_one.shape[1]
    gate_one = gate_one.reshape(n, -1, wide)
    down_one = down_one.reshape(n, -1, down_one.shape[1])
    blocks = [gate_one]
    for at in range(0, down_one.shape[2], wide):
        block = down_one[:, :, at : at + wide]
        short = wide - block.shape[2]
        blocks.append(jnp.pad(block, ((0, 0), (0, 0), (0, short))) if short else block)
    return jnp.concatenate(blocks, axis=1)


def unpack(piece, gate_rows, down_rows, down_width):
    blocks = [
        piece[at : at + down_rows] for at in range(gate_rows, piece.shape[0], down_rows)
    ]
    return piece[:gate_rows], jnp.concatenate(blocks, axis=1)[:, :down_width]


def split3(x):
    hi = lax.reduce_precision(x, 8, 7)
    mid = lax.reduce_precision(x - hi, 8, 7)
    lo = x - hi - mid
    return [v.astype(BF) for v in (hi, mid, lo)]


def glu(gate_up):
    half = gate_up.shape[-2] // 2
    return (jax.nn.silu(gate_up[..., :half, :]) * gate_up[..., half:, :]).astype(BF)


def per_device(
    tokens,
    route_ids,
    route_weights,
    placement,
    gate_up,
    down,
    queries,
    draft_keys,
    draft_values,
    cache_keys,
    cache_values,
    cache_lengths,
):
    n_dp, n_x = lax.axis_size("dp"), lax.axis_size("x")
    n_expert = lax.axis_size(PLANE)
    me, here = lax.axis_index("dp"), lax.axis_index(PLANE)
    core = lax.axis_index("core")
    rows, picks = route_ids.shape
    slots = placement.shape[0]
    per = gate_up.shape[0]
    width = tokens.shape[1]
    part = width // n_dp
    quarter = gate_up.shape[2] // 2
    chunk = n_dp * CAP
    all_rows = n_dp * rows
    slot_range = jnp.arange(slots, dtype=jnp.int32)
    ks, xs = range(n_dp), range(n_x)

    def plane(k):
        return (me + n_dp - k) % n_dp

    slot_of = jnp.sum(
        jnp.where(route_ids[:, :, None] == slot_range, placement, 0), axis=2
    )
    info = jnp.concatenate([slot_of.astype(BF)] + split3(route_weights), axis=1)
    info = jnp.pad(info, ((0, 0), (0, LANES - info.shape[1])))
    sent = jnp.concatenate([tokens, info], axis=1)
    came = [ring(sent, "dp", k) for k in ks]
    came_tokens = [x[:, :width] for x in came]
    infos = jnp.concatenate([x[:, width:] for x in came], axis=0)
    my_part = jnp.concatenate(
        [lax.dynamic_slice_in_dim(x, me * part, part, axis=1) for x in came_tokens], axis=0
    )

    own = jnp.sum(slot_of[:, :, None] == slot_range, axis=(0, 1))
    hot = own > CAP
    first_hot = jnp.min(jnp.where(hot, slot_range, slots - 1))
    last_hot = jnp.max(jnp.where(hot, slot_range, 0))
    my_hot = jnp.where(core == 0, first_hot, last_hot)
    other_hot = jnp.where(core == 0, last_hot, first_hot)

    owner = my_hot // per

    def packed(slot):
        return pack(
            lax.dynamic_index_in_dim(gate_up, slot % per, 0, keepdims=False),
            lax.dynamic_index_in_dim(down, slot % per, 0, keepdims=False),
            n_x,
        )

    theirs = swap(packed(other_hot))
    held = jnp.where(owner == here, packed(my_hot), theirs)
    held = jnp.where(owner // 2 == here // 2, held, 0.0)
    piece = lax.psum_scatter(held, "x", scatter_dimension=0, tiled=False)

    to_send = [
        lax.dynamic_slice_in_dim(gate_up, (me + k) % n_dp * part, part, axis=1) for k in ks
    ]
    pieces = [ring(x, "dp", k) for k, x in zip(ks, to_send)]

    match = infos[:, :picks].astype(jnp.int32)[:, :, None] == slot_range
    came_weights = sum(infos[:, i * picks : (i + 1) * picks].astype(F32) for i in (1, 2, 3))
    takes = jnp.any(match, axis=1)
    weight_of = jnp.sum(jnp.where(match, came_weights[:, :, None], 0.0), axis=1)
    takes_plane = takes.reshape(n_dp, rows, slots).astype(jnp.int32)
    rank = (jnp.cumsum(takes_plane, axis=1) - takes_plane).reshape(all_rows, slots)
    plane_of = (me + n_dp - jnp.arange(all_rows, dtype=jnp.int32) // rows) % n_dp
    code = jnp.where(takes & ~hot[None, :], plane_of[:, None] * CAP + rank, -1)
    place = code.T[:, None, :] == jnp.arange(chunk, dtype=jnp.int32)[None, :, None]
    place = place.reshape(slots * chunk, all_rows)
    combine = jnp.where(place, jnp.repeat(weight_of.T, chunk, axis=0), 0.0)
    combine = jnp.concatenate(split3(combine), axis=1)

    outgoing = dot(after(place.astype(BF), held, *to_send), my_part, ((1,), (0,))).astype(BF)
    arrived = lax.all_to_all(
        outgoing.reshape(n_expert, per * chunk, part), PLANE, 0, 0, tiled=True
    )
    xs_in = [
        arrived[:, s * chunk : (s + 1) * chunk].reshape(n_expert * chunk, part)
        for s in range(per)
    ]
    pieces[-1] = after(pieces[-1], piece)

    def partial(k):
        return jnp.concatenate([dot(x, w, ((1,), (0,))) for x, w in zip(xs_in, pieces[k])])

    total = partial(0)
    for k in ks[1:]:
        total = total + ring(partial(k).astype(BF), "dp", -k).astype(F32)
    hidden = jax.nn.silu(total[:, :quarter]) * total[:, quarter:]
    hidden = jnp.swapaxes(hidden.astype(BF).reshape(per, -1, quarter), 1, 2)
    outs = [0.0] * per
    for k in ks:
        hidden_k = ring(hidden, "dp", k)
        for s in range(per):
            down_piece = lax.dynamic_slice_in_dim(down[s], plane(k) * quarter, quarter, axis=0)
            outs[s] = outs[s] + dot(hidden_k[s], down_piece, ((0,), (0,)))
    out = jnp.concatenate([o.astype(BF).reshape(n_expert, chunk, part) for o in outs], axis=1)
    back = lax.all_to_all(out, PLANE, 0, 0, tiled=True).reshape(slots * chunk, part)

    piece = after(lax.psum(piece, "z"), out)
    slices = lax.all_gather(piece, "x", axis=0)
    hot_pieces = [
        unpack(slices[i], width // n_x, down.shape[1] // n_x, part) for i in range(n_x)
    ]
    all_tokens = jnp.zeros((all_rows, width), BF)
    for k in ks:
        all_tokens = lax.dynamic_update_slice_in_dim(
            all_tokens, came_tokens[k], plane(k) * rows, axis=0
        )
    both_tokens = jnp.concatenate([all_tokens, swap(all_tokens)], axis=0)
    gated = 0.0
    for k in xs:
        size = width // n_x
        some = both_tokens[:, k * size : (k + 1) * size]
        gated = gated + dot(hot_pieces[k][0], some, ((0,), (1,)))
    hidden_hot = glu(gated)
    hidden_all = jnp.zeros((n_dp * quarter, 2 * all_rows), BF)
    for k in ks:
        hidden_all = lax.dynamic_update_slice_in_dim(
            hidden_all, ring(hidden_hot, "dp", k), plane(k) * quarter, axis=0
        )
    hot_out = 0.0
    for k in xs:
        size = hidden_all.shape[0] // n_x
        some = hidden_all[k * size : (k + 1) * size]
        hot_out = hot_out + dot(some, hot_pieces[k][1], ((0,), (0,)))
    hot_out = hot_out.astype(BF)
    from_sibling = swap(hot_out[all_rows:])

    mixed = dot(combine, back, ((0,), (0,)))
    mixed = mixed[:all_rows] + mixed[all_rows : 2 * all_rows] + mixed[2 * all_rows :]
    for one, out in ((my_hot, hot_out[:all_rows]), (other_hot, from_sibling)):
        hot_weight = jnp.sum(jnp.where(slot_range == one, weight_of, 0.0), axis=1)
        out = jnp.concatenate(
            [lax.dynamic_slice_in_dim(out, plane(k) * rows, rows) for k in ks]
        )
        mixed = mixed + hot_weight[:, None] * out.astype(F32)

    mixed = mixed.astype(BF).reshape(n_dp, rows, part)
    mixed_out = jnp.zeros((rows, width), BF)
    for k in ks:
        mixed_out = lax.dynamic_update_slice_in_dim(
            mixed_out, ring(mixed[k], "dp", -k), (me + k) % n_dp * part, axis=1
        )
    context = attend_block(
        after(queries, hidden), draft_keys, draft_values, cache_keys, cache_values, cache_lengths
    )
    return (mixed_out, context)


def solution(mesh):
    chips = Mesh(mesh.devices.reshape(mesh.shape["dp"], 4, -1, 2), ALL)
    in_specs = (
        P(ALL, None),
        P(ALL, None),
        P(ALL, None),
        P(),
        P(PLANE, None, "dp"),
        P(PLANE, None, "dp"),
        P(ALL, None, None),
        P(ALL, None, None),
        P(ALL, None, None),
        P(ALL, None, None),
        P(ALL, None, None),
        P(ALL),
    )
    out_specs = (P(ALL, None), P(ALL, None, None))
    return jax.shard_map(
        per_device, mesh=chips, in_specs=in_specs, out_specs=out_specs, check_vma=False
    )
```

```python
import functools
import math

import jax
import jax.numpy as jnp
from jax import lax
from jax.experimental import pallas as pl
from jax.experimental.pallas import tpu as pltpu
from jax.sharding import Mesh
from jax.sharding import PartitionSpec as P

HEAD_DIM = 128
HOT = 2
CAP = 2
HOT_ROWS = 4
LANES = 128
PLANE = ("x", "z", "core")
ALL = ("dp",) + PLANE
BF = jnp.bfloat16
F32 = jnp.float32


def attend_block(queries, draft_keys, draft_values, cache_keys, cache_values, cache_lengths):
    req_here, drafts, query_width = queries.shape
    context_len = cache_keys.shape[1]
    groups = draft_keys.shape[2] // HEAD_DIM
    per_group = query_width // (groups * HEAD_DIM)
    scaling = 1.0 / math.sqrt(HEAD_DIM)
    query_heads = queries.reshape(req_here, drafts, groups, per_group, HEAD_DIM)
    cache_k = cache_keys.reshape(req_here, context_len, groups, HEAD_DIM)
    cache_v = cache_values.reshape(req_here, context_len, groups, HEAD_DIM)
    draft_k = draft_keys.reshape(req_here, drafts, groups, HEAD_DIM)
    draft_v = draft_values.reshape(req_here, drafts, groups, HEAD_DIM)
    score_cache = (
        jnp.einsum("rigpe,rcge->rgpic", query_heads, cache_k, preferred_element_type=jnp.float32)
        * scaling
    )
    score_draft = (
        jnp.einsum("rigpe,rjge->rgpij", query_heads, draft_k, preferred_element_type=jnp.float32)
        * scaling
    )
    live_cache = jnp.arange(context_len, dtype=jnp.int32)[None, :] < cache_lengths[:, None]
    live_draft = (
        jnp.arange(drafts, dtype=jnp.int32)[None, :] <= jnp.arange(drafts, dtype=jnp.int32)[:, None]
    )
    score_cache = jnp.where(live_cache[:, None, None, None, :], score_cache, -1e30)
    score_draft = jnp.where(live_draft[None, None, None, :, :], score_draft, -1e30)
    highest = jnp.maximum(jnp.max(score_cache, axis=-1), jnp.max(score_draft, axis=-1))
    expo_cache = jnp.exp(score_cache - highest[..., None])
    expo_draft = jnp.exp(score_draft - highest[..., None])
    totals = jnp.sum(expo_cache, axis=-1) + jnp.sum(expo_draft, axis=-1)
    prob_cache = (expo_cache / totals[..., None]).astype(jnp.bfloat16)
    prob_draft = (expo_draft / totals[..., None]).astype(jnp.bfloat16)
    result = jnp.einsum(
        "rgpic,rcge->rigpe", prob_cache, cache_v, preferred_element_type=jnp.float32
    )
    result = result + jnp.einsum(
        "rgpij,rjge->rigpe", prob_draft, draft_v, preferred_element_type=jnp.float32
    )
    return result.astype(jnp.bfloat16).reshape(req_here, drafts, query_width)


def ring(x, axis, k, n=4):
    k = k % n
    return x if k == 0 else lax.ppermute(x, axis, [(i, (i + k) % n) for i in range(n)])


def swap(x):
    return lax.ppermute(x, "core", [(0, 1), (1, 0)])


def after(x, *others):
    return lax.optimization_barrier((x, *others))[0]


def dot(a, b, dims, batch=()):
    return lax.dot_general(a, b, (dims, (batch, batch)), preferred_element_type=F32)


def split3(x):
    hi = lax.reduce_precision(x, 8, 7)
    mid = lax.reduce_precision(x - hi, 8, 7)
    lo = x - hi - mid
    return [v.astype(BF) for v in (hi, mid, lo)]


def place_kernel(picks, info_ref, hot_ref, plane_ref, rows_ref, out_ref, combine_ref, rank_ref):
    info = info_ref[...].astype(F32)
    tokens, slots = info.shape[0], hot_ref.shape[1]
    rows = tokens // 4
    chunk = out_ref.shape[0] // slots
    lane = lax.broadcasted_iota(jnp.int32, (tokens, slots), 1).astype(F32)
    takes = jnp.zeros((tokens, slots), F32)
    weights = [jnp.zeros((tokens, slots), F32) for _ in range(3)]
    for k in range(picks):
        match = lane == info[:, k : k + 1]
        takes = jnp.where(match, 1.0, takes)
        for i in range(3):
            at = (i + 1) * picks + k
            weights[i] = jnp.where(match, info[:, at : at + 1], weights[i])
    early = lax.broadcasted_iota(jnp.int32, (tokens, tokens), 1)
    late = lax.broadcasted_iota(jnp.int32, (tokens, tokens), 0)
    before = late > early
    for k in range(1, 4):
        before = before & ((late >= k * rows) == (early >= k * rows))
    rank = jnp.dot(
        before.astype(BF), takes.astype(BF), preferred_element_type=F32
    )
    rank_ref[...] = jnp.where(takes > 0, rank, -1.0)
    cold = (takes > 0) & (hot_ref[...] == 0)
    code = jnp.where(cold, plane_ref[...] * CAP + rank, -1.0)
    wide = slots * chunk
    slot_at = lax.broadcasted_iota(jnp.int32, (slots, wide), 0)
    column = lax.broadcasted_iota(jnp.int32, (slots, wide), 1)
    spread = (column // chunk == slot_at).astype(BF)
    code = jnp.dot(code.astype(BF), spread, preferred_element_type=F32)
    turn = lax.broadcasted_iota(jnp.int32, (tokens, wide), 1) % chunk
    place = code == turn.astype(F32)
    for i in range(3):
        spread_weight = jnp.dot(weights[i].astype(BF), spread, preferred_element_type=F32)
        combine_ref[i] = jnp.where(place, spread_weight, 0.0).astype(BF)
    out_ref[...] = lax.dot_general(
        place.astype(BF), rows_ref[...], (((0,), (0,)), ((), ())), preferred_element_type=F32
    ).astype(BF)


def place_rows(infos, hot, planes, my_part, picks, chunk):
    tokens, part = my_part.shape
    slots = hot.shape[1]
    return pl.pallas_call(
        functools.partial(place_kernel, picks),
        out_shape=(
            jax.ShapeDtypeStruct((slots * chunk, part), BF),
            jax.ShapeDtypeStruct((3, tokens, slots * chunk), BF),
            jax.ShapeDtypeStruct((tokens, slots), F32),
        ),
        compiler_params=pltpu.CompilerParams(vmem_limit_bytes=32 * 2**20),
        cost_estimate=pl.CostEstimate(
            flops=60_000_000_000, bytes_accessed=200_000_000, transcendentals=0
        ),
    )(infos, hot, planes, my_part)


def per_device(
    tokens,
    route_ids,
    route_weights,
    placement,
    gate_up,
    down,
    queries,
    draft_keys,
    draft_values,
    cache_keys,
    cache_values,
    cache_lengths,
):
    n_dp, n_x = lax.axis_size("dp"), lax.axis_size("x")
    n_expert = lax.axis_size(PLANE)
    me, here = lax.axis_index("dp"), lax.axis_index(PLANE)
    here_x, core = lax.axis_index("x"), lax.axis_index("core")
    rows, picks = route_ids.shape
    slots = placement.shape[0]
    per = gate_up.shape[0]
    width = tokens.shape[1]
    part = width // n_dp
    quarter = gate_up.shape[2] // 2
    chunk = n_dp * CAP
    all_rows = n_dp * rows
    slot_range = jnp.arange(slots, dtype=jnp.int32)
    ks, xs = range(n_dp), range(n_x)

    def plane(k):
        return (me + n_dp - k) % n_dp

    slot_of = jnp.sum(
        jnp.where(route_ids[:, :, None] == slot_range, placement, 0), axis=2
    )
    info = jnp.concatenate([slot_of.astype(BF)] + split3(route_weights), axis=1)
    info = jnp.pad(info, ((0, 0), (0, LANES - info.shape[1])))
    sent = jnp.concatenate([tokens, info], axis=1)
    came = [ring(sent, "dp", k) for k in ks]
    came_tokens = [x[:, :width] for x in came]
    infos = jnp.concatenate([x[:, width:] for x in came], axis=0)
    my_part = jnp.concatenate(
        [lax.dynamic_slice_in_dim(x, me * part, part, axis=1) for x in came_tokens], axis=0
    )

    own = jnp.sum(slot_of[:, :, None] == slot_range, axis=(0, 1))
    hot = own > CAP
    first_hot = jnp.min(jnp.where(hot, slot_range, slots - 1))
    last_hot = jnp.max(jnp.where(hot, slot_range, 0))
    my_hot = jnp.where(core == 0, first_hot, last_hot)
    other_hot = jnp.where(core == 0, last_hot, first_hot)

    owner = my_hot // per

    def on_owner(weights):
        theirs = swap(lax.dynamic_index_in_dim(weights, other_hot % per, 0, keepdims=False))
        mine = lax.dynamic_index_in_dim(weights, my_hot % per, 0, keepdims=False)
        return jnp.where(owner == here, mine, jnp.where(owner == here + 1 - 2 * core, theirs, 0.0))

    held = (on_owner(gate_up), on_owner(down))
    piece = lax.psum_scatter(held, "x", scatter_dimension=0, tiled=True)

    to_send = [
        lax.dynamic_slice_in_dim(gate_up, (me + k) % n_dp * part, part, axis=1) for k in ks
    ]
    pieces = [ring(x, "dp", k) for k, x in zip(ks, to_send)]

    plane_of = (me + n_dp - jnp.arange(all_rows, dtype=jnp.int32) // rows) % n_dp
    planes = plane_of.astype(F32)[:, None]
    my_part, *_ = lax.optimization_barrier((my_part, *held, *to_send))
    outgoing, combine, rank_of = place_rows(
        infos, hot[None, :].astype(jnp.int32), planes, my_part, picks, chunk
    )
    arrived = lax.all_to_all(
        outgoing.reshape(n_expert, per * chunk, part), PLANE, 0, 0, tiled=True
    )
    xs_in = [
        arrived[:, s * chunk : (s + 1) * chunk].reshape(n_expert * chunk, part)
        for s in range(per)
    ]
    pieces[-1] = after(pieces[-1], *piece)

    def partial(k):
        return jnp.concatenate([dot(x, w, ((1,), (0,))) for x, w in zip(xs_in, pieces[k])])

    total = partial(0)
    for k in ks[1:]:
        total = total + ring(partial(k).astype(BF), "dp", -k).astype(F32)
    hidden = jax.nn.silu(total[:, :quarter]) * total[:, quarter:]
    hidden = jnp.swapaxes(hidden.astype(BF).reshape(per, -1, quarter), 1, 2)
    outs = [0.0] * per
    for k in ks:
        hidden_k = ring(hidden, "dp", k)
        for s in range(per):
            down_piece = lax.dynamic_slice_in_dim(down[s], plane(k) * quarter, quarter, axis=0)
            outs[s] = outs[s] + dot(hidden_k[s], down_piece, ((0,), (0,)))
    out = jnp.concatenate([o.astype(BF).reshape(n_expert, chunk, part) for o in outs], axis=1)
    back = lax.all_to_all(out, PLANE, 0, 0, tiled=True).reshape(slots * chunk, part)

    came_slots = infos[:, :picks].astype(jnp.int32)
    came_weights = sum(infos[:, i * picks : (i + 1) * picks].astype(F32) for i in (1, 2, 3))

    def hot_rows_of(slot):
        rank = jnp.sum(jnp.where(slot_range == slot, rank_of, 0.0), axis=1).astype(jnp.int32)
        code = jnp.where(rank >= 0, plane_of * HOT_ROWS + rank, -1)
        find = code[None, :] == jnp.arange(n_dp * HOT_ROWS, dtype=jnp.int32)[:, None]
        weight = jnp.sum(jnp.where(came_slots == slot, came_weights, 0.0), axis=1)
        return find, jnp.where(find, weight, 0.0)

    came_all = jnp.concatenate(came_tokens, axis=0)
    find_mine, weigh_mine = hot_rows_of(my_hot)
    find_other, weigh_other = hot_rows_of(other_hot)
    half = n_dp * HOT_ROWS
    found = dot(jnp.concatenate([find_mine, find_other]).astype(BF), came_all, ((1,), (0,)))
    found = after(found.astype(BF), arrived)
    found = jnp.concatenate([found[:half], swap(found[half:])])

    def of_x(x, k, axis):
        size = x.shape[axis] // n_x
        return lax.dynamic_slice_in_dim(x, (here_x + k) % n_x * size, size, axis=axis)

    def back_to_x(x):
        size = x.shape[0] // n_x
        total = x[:size]
        for k in xs[1:]:
            sent_back = x[k * size : (k + 1) * size].astype(BF)
            total = total + ring(sent_back, "x", -k).astype(F32)
        return total

    x_rows = jnp.concatenate([ring(of_x(found, k, 1), "x", k) for k in xs])
    hot_gate, hot_down = lax.psum(piece, "z")
    hot_gate, hot_down, _ = lax.optimization_barrier((hot_gate, hot_down, out))
    gated = back_to_x(dot(x_rows, hot_gate, ((1,), (0,))))
    hidden_hot = (jax.nn.silu(gated[:, :quarter]) * gated[:, quarter:]).astype(BF)
    hidden_all = jnp.zeros((n_dp * 2 * half, quarter), BF)
    for k in ks:
        hidden_all = lax.dynamic_update_slice_in_dim(
            hidden_all, ring(hidden_hot, "dp", k), plane(k) * 2 * half, axis=0
        )
    x_hidden = jnp.concatenate([ring(of_x(hidden_all, k, 0), "x", k) for k in xs])
    hot_out = back_to_x(dot(x_hidden, hot_down, ((1,), (0,)))).astype(BF)
    hot_outs = jnp.concatenate([hot_out[:half], swap(hot_out[half:])])
    weigh = jnp.concatenate([weigh_mine, weigh_other])

    mixed = dot(combine[0], back, ((1,), (0,)))
    for i in (1, 2):
        mixed = mixed + dot(combine[i], back, ((1,), (0,)))
    for weigh_i in split3(weigh):
        mixed = mixed + dot(weigh_i, hot_outs, ((0,), (0,)))

    mixed = mixed.astype(BF).reshape(n_dp, rows, part)
    mixed_out = jnp.zeros((rows, width), BF)
    for k in ks:
        mixed_out = lax.dynamic_update_slice_in_dim(
            mixed_out, ring(mixed[k], "dp", -k), (me + k) % n_dp * part, axis=1
        )
    context = attend_block(
        after(queries, hidden), draft_keys, draft_values, cache_keys, cache_values, cache_lengths
    )
    return (mixed_out, context)


def solution(mesh):
    chips = Mesh(mesh.devices.reshape(mesh.shape["dp"], 4, -1, 2), ALL)
    in_specs = (
        P(ALL, None),
        P(ALL, None),
        P(ALL, None),
        P(),
        P(PLANE, None, "dp"),
        P(PLANE, None, "dp"),
        P(ALL, None, None),
        P(ALL, None, None),
        P(ALL, None, None),
        P(ALL, None, None),
        P(ALL, None, None),
        P(ALL),
    )
    out_specs = (P(ALL, None), P(ALL, None, None))
    return jax.shard_map(
        per_device, mesh=chips, in_specs=in_specs, out_specs=out_specs, check_vma=False
    )
```

```python
import functools
import math

import jax
import jax.numpy as jnp
from jax import lax
from jax.experimental import pallas as pl
from jax.experimental.pallas import tpu as pltpu
from jax.sharding import Mesh
from jax.sharding import PartitionSpec as P

HEAD_DIM = 128
HOT = 2
CAP = 2
HOT_ROWS = 4
LANES = 128
PLANE = ("x", "z", "core")
ALL = ("dp",) + PLANE
BF = jnp.bfloat16
F32 = jnp.float32


def attend_block(queries, draft_keys, draft_values, cache_keys, cache_values, cache_lengths):
    req_here, drafts, query_width = queries.shape
    context_len = cache_keys.shape[1]
    groups = draft_keys.shape[2] // HEAD_DIM
    per_group = query_width // (groups * HEAD_DIM)
    scaling = 1.0 / math.sqrt(HEAD_DIM)
    query_heads = queries.reshape(req_here, drafts, groups, per_group, HEAD_DIM)
    cache_k = cache_keys.reshape(req_here, context_len, groups, HEAD_DIM)
    cache_v = cache_values.reshape(req_here, context_len, groups, HEAD_DIM)
    draft_k = draft_keys.reshape(req_here, drafts, groups, HEAD_DIM)
    draft_v = draft_values.reshape(req_here, drafts, groups, HEAD_DIM)
    score_cache = (
        jnp.einsum("rigpe,rcge->rgpic", query_heads, cache_k, preferred_element_type=jnp.float32)
        * scaling
    )
    score_draft = (
        jnp.einsum("rigpe,rjge->rgpij", query_heads, draft_k, preferred_element_type=jnp.float32)
        * scaling
    )
    live_cache = jnp.arange(context_len, dtype=jnp.int32)[None, :] < cache_lengths[:, None]
    live_draft = (
        jnp.arange(drafts, dtype=jnp.int32)[None, :] <= jnp.arange(drafts, dtype=jnp.int32)[:, None]
    )
    score_cache = jnp.where(live_cache[:, None, None, None, :], score_cache, -1e30)
    score_draft = jnp.where(live_draft[None, None, None, :, :], score_draft, -1e30)
    highest = jnp.maximum(jnp.max(score_cache, axis=-1), jnp.max(score_draft, axis=-1))
    expo_cache = jnp.exp(score_cache - highest[..., None])
    expo_draft = jnp.exp(score_draft - highest[..., None])
    totals = jnp.sum(expo_cache, axis=-1) + jnp.sum(expo_draft, axis=-1)
    prob_cache = (expo_cache / totals[..., None]).astype(jnp.bfloat16)
    prob_draft = (expo_draft / totals[..., None]).astype(jnp.bfloat16)
    result = jnp.einsum(
        "rgpic,rcge->rigpe", prob_cache, cache_v, preferred_element_type=jnp.float32
    )
    result = result + jnp.einsum(
        "rgpij,rjge->rigpe", prob_draft, draft_v, preferred_element_type=jnp.float32
    )
    return result.astype(jnp.bfloat16).reshape(req_here, drafts, query_width)


def ring(x, axis, k, n=4):
    k = k % n
    return x if k == 0 else lax.ppermute(x, axis, [(i, (i + k) % n) for i in range(n)])


def swap(x):
    return lax.ppermute(x, "core", [(0, 1), (1, 0)])


def after(x, *others):
    return lax.optimization_barrier((x, *others))[0]


def dot(a, b, dims, batch=()):
    return lax.dot_general(a, b, (dims, (batch, batch)), preferred_element_type=F32)


def split3(x):
    hi = lax.reduce_precision(x, 8, 7)
    mid = lax.reduce_precision(x - hi, 8, 7)
    lo = x - hi - mid
    return [v.astype(BF) for v in (hi, mid, lo)]


def settle_kernel(x_ref, out_ref):
    pass


def settle(x, micros):
    return pl.pallas_call(
        settle_kernel,
        out_shape=jax.ShapeDtypeStruct(x.shape, x.dtype),
        in_specs=[pl.BlockSpec(memory_space=pl.ANY)],
        out_specs=pl.BlockSpec(memory_space=pl.ANY),
        input_output_aliases={0: 0},
        cost_estimate=pl.CostEstimate(
            flops=micros * 1_000_000_000, bytes_accessed=micros * 3_000_000, transcendentals=0
        ),
    )(x)


def partial_kernel(x_ref, w_ref, out_ref):
    sources, lines, part = x_ref.shape
    per = w_ref.shape[0]
    chunk = lines // per
    x = x_ref[...].reshape(sources * lines, part)
    for s in range(per):
        y = jnp.dot(x, w_ref[s], preferred_element_type=F32).reshape(sources, lines, -1)
        y = y[:, s * chunk : (s + 1) * chunk].reshape(sources * chunk, -1)
        out_ref[pl.ds(s * sources * chunk, sources * chunk), :] = y.astype(out_ref.dtype)


def partial_sums(arrived, weights, dtype):
    sources, lines, part = arrived.shape
    return pl.pallas_call(
        partial_kernel,
        out_shape=jax.ShapeDtypeStruct((sources * lines, weights.shape[2]), dtype),
        compiler_params=pltpu.CompilerParams(vmem_limit_bytes=48 * 2**20),
        cost_estimate=pl.CostEstimate(
            flops=2 * sources * lines * part * weights.shape[2],
            bytes_accessed=2 * (arrived.size + weights.size),
            transcendentals=0,
        ),
    )(arrived, weights)


def place_kernel(picks, info_ref, hot_ref, plane_ref, rows_ref, out_ref, combine_ref, rank_ref):
    info = info_ref[...].astype(F32)
    tokens, slots = info.shape[0], hot_ref.shape[1]
    rows = tokens // 4
    chunk = out_ref.shape[0] // slots
    lane = lax.broadcasted_iota(jnp.int32, (tokens, slots), 1).astype(F32)
    takes = jnp.zeros((tokens, slots), F32)
    weights = [jnp.zeros((tokens, slots), F32) for _ in range(3)]
    for k in range(picks):
        match = lane == info[:, k : k + 1]
        takes = jnp.where(match, 1.0, takes)
        for i in range(3):
            at = (i + 1) * picks + k
            weights[i] = jnp.where(match, info[:, at : at + 1], weights[i])
    early = lax.broadcasted_iota(jnp.int32, (tokens, tokens), 1)
    late = lax.broadcasted_iota(jnp.int32, (tokens, tokens), 0)
    before = late > early
    for k in range(1, 4):
        before = before & ((late >= k * rows) == (early >= k * rows))
    rank = jnp.dot(
        before.astype(BF), takes.astype(BF), preferred_element_type=F32
    )
    rank_ref[...] = jnp.where(takes > 0, rank, -1.0)
    cold = (takes > 0) & (hot_ref[...] == 0)
    code = jnp.where(cold, plane_ref[...] * CAP + rank, -1.0)
    wide = slots * chunk
    slot_at = lax.broadcasted_iota(jnp.int32, (slots, wide), 0)
    column = lax.broadcasted_iota(jnp.int32, (slots, wide), 1)
    spread = (column // chunk == slot_at).astype(BF)
    code = jnp.dot(code.astype(BF), spread, preferred_element_type=F32)
    turn = lax.broadcasted_iota(jnp.int32, (tokens, wide), 1) % chunk
    place = code == turn.astype(F32)
    for i in range(3):
        spread_weight = jnp.dot(weights[i].astype(BF), spread, preferred_element_type=F32)
        combine_ref[i] = jnp.where(place, spread_weight, 0.0).astype(BF)
    out_ref[...] = lax.dot_general(
        place.astype(BF), rows_ref[...], (((0,), (0,)), ((), ())), preferred_element_type=F32
    ).astype(BF)


def place_rows(infos, hot, planes, my_part, picks, chunk):
    tokens, part = my_part.shape
    slots = hot.shape[1]
    return pl.pallas_call(
        functools.partial(place_kernel, picks),
        out_shape=(
            jax.ShapeDtypeStruct((slots * chunk, part), BF),
            jax.ShapeDtypeStruct((3, tokens, slots * chunk), BF),
            jax.ShapeDtypeStruct((tokens, slots), F32),
        ),
        compiler_params=pltpu.CompilerParams(vmem_limit_bytes=32 * 2**20),
        cost_estimate=pl.CostEstimate(
            flops=1_000_000_000, bytes_accessed=4_000_000, transcendentals=0
        ),
    )(infos, hot, planes, my_part)


def per_device(
    tokens,
    route_ids,
    route_weights,
    placement,
    gate_up,
    down,
    queries,
    draft_keys,
    draft_values,
    cache_keys,
    cache_values,
    cache_lengths,
):
    n_dp, n_x = lax.axis_size("dp"), lax.axis_size("x")
    n_expert = lax.axis_size(PLANE)
    me, here = lax.axis_index("dp"), lax.axis_index(PLANE)
    here_x, core = lax.axis_index("x"), lax.axis_index("core")
    rows, picks = route_ids.shape
    slots = placement.shape[0]
    per = gate_up.shape[0]
    width = tokens.shape[1]
    part = width // n_dp
    quarter = gate_up.shape[2] // 2
    chunk = n_dp * CAP
    all_rows = n_dp * rows
    slot_range = jnp.arange(slots, dtype=jnp.int32)
    ks, xs = range(n_dp), range(n_x)

    def plane(k):
        return (me + n_dp - k) % n_dp

    slot_of = jnp.sum(
        jnp.where(route_ids[:, :, None] == slot_range, placement, 0), axis=2
    )
    info = jnp.concatenate([slot_of.astype(BF)] + split3(route_weights), axis=1)
    info = jnp.pad(info, ((0, 0), (0, LANES - info.shape[1])))
    sent = jnp.concatenate([tokens, info], axis=1)
    came = [ring(sent, "dp", k) for k in ks]
    came_tokens = [x[:, :width] for x in came]
    infos = jnp.concatenate([x[:, width:] for x in came], axis=0)
    my_part = jnp.concatenate(
        [lax.dynamic_slice_in_dim(x, me * part, part, axis=1) for x in came_tokens], axis=0
    )

    own = jnp.sum(slot_of[:, :, None] == slot_range, axis=(0, 1))
    hot = own > CAP
    first_hot = jnp.min(jnp.where(hot, slot_range, slots - 1))
    last_hot = jnp.max(jnp.where(hot, slot_range, 0))
    my_hot = jnp.where(core == 0, first_hot, last_hot)
    other_hot = jnp.where(core == 0, last_hot, first_hot)

    owner = my_hot // per

    def on_owner(weights):
        theirs = swap(lax.dynamic_index_in_dim(weights, other_hot % per, 0, keepdims=False))
        mine = lax.dynamic_index_in_dim(weights, my_hot % per, 0, keepdims=False)
        return jnp.where(owner == here, mine, jnp.where(owner == here + 1 - 2 * core, theirs, 0.0))

    held = (on_owner(gate_up), on_owner(down))
    piece = lax.psum_scatter(held, "x", scatter_dimension=0, tiled=True)

    to_send = [
        lax.dynamic_slice_in_dim(gate_up, (me + k) % n_dp * part, part, axis=1) for k in ks
    ]
    pieces = [ring(x, "dp", k) for k, x in zip(ks, to_send)]

    plane_of = (me + n_dp - jnp.arange(all_rows, dtype=jnp.int32) // rows) % n_dp
    planes = plane_of.astype(F32)[:, None]
    my_part, *_ = lax.optimization_barrier((my_part, *held, *to_send))
    outgoing, combine, rank_of = place_rows(
        infos, hot[None, :].astype(jnp.int32), planes, my_part, picks, chunk
    )
    arrived = lax.all_to_all(
        outgoing.reshape(n_expert, per * chunk, part), PLANE, 0, 0, tiled=True
    )
    pieces[-1] = after(pieces[-1], *piece)

    pieces[2] = settle(pieces[2], 40)
    total = partial_sums(arrived, pieces[0], F32)
    for k in ks[1:]:
        total = total + ring(partial_sums(arrived, pieces[k], BF), "dp", -k).astype(F32)
    hidden = jax.nn.silu(total[:, :quarter]) * total[:, quarter:]
    hidden = jnp.swapaxes(hidden.astype(BF).reshape(per, -1, quarter), 1, 2)
    outs = [0.0] * per
    for k in ks:
        hidden_k = ring(hidden, "dp", k)
        for s in range(per):
            down_piece = lax.dynamic_slice_in_dim(down[s], plane(k) * quarter, quarter, axis=0)
            outs[s] = outs[s] + dot(hidden_k[s], down_piece, ((0,), (0,)))
    out = jnp.concatenate([o.astype(BF).reshape(n_expert, chunk, part) for o in outs], axis=1)
    back = lax.all_to_all(out, PLANE, 0, 0, tiled=True).reshape(slots * chunk, part)

    came_slots = infos[:, :picks].astype(jnp.int32)
    came_weights = sum(infos[:, i * picks : (i + 1) * picks].astype(F32) for i in (1, 2, 3))

    def hot_rows_of(slot):
        rank = jnp.sum(jnp.where(slot_range == slot, rank_of, 0.0), axis=1).astype(jnp.int32)
        code = jnp.where(rank >= 0, plane_of * HOT_ROWS + rank, -1)
        find = code[None, :] == jnp.arange(n_dp * HOT_ROWS, dtype=jnp.int32)[:, None]
        weight = jnp.sum(jnp.where(came_slots == slot, came_weights, 0.0), axis=1)
        return find, jnp.where(find, weight, 0.0)

    came_all = jnp.concatenate(came_tokens, axis=0)
    find_mine, weigh_mine = hot_rows_of(my_hot)
    find_other, weigh_other = hot_rows_of(other_hot)
    half = n_dp * HOT_ROWS
    found = dot(jnp.concatenate([find_mine, find_other]).astype(BF), came_all, ((1,), (0,)))
    found = after(found.astype(BF), arrived)
    found = jnp.concatenate([found[:half], swap(found[half:])])

    def of_x(x, k, axis):
        size = x.shape[axis] // n_x
        return lax.dynamic_slice_in_dim(x, (here_x + k) % n_x * size, size, axis=axis)

    def back_to_x(x):
        size = x.shape[0] // n_x
        total = x[:size]
        for k in xs[1:]:
            sent_back = x[k * size : (k + 1) * size].astype(BF)
            total = total + ring(sent_back, "x", -k).astype(F32)
        return total

    x_rows = jnp.concatenate([ring(of_x(found, k, 1), "x", k) for k in xs])
    hot_gate, hot_down = lax.psum(piece, "z")
    hot_gate, hot_down, _ = lax.optimization_barrier((hot_gate, hot_down, out))
    gated = back_to_x(dot(x_rows, hot_gate, ((1,), (0,))))
    hidden_hot = (jax.nn.silu(gated[:, :quarter]) * gated[:, quarter:]).astype(BF)
    hidden_all = jnp.zeros((n_dp * 2 * half, quarter), BF)
    for k in ks:
        hidden_all = lax.dynamic_update_slice_in_dim(
            hidden_all, ring(hidden_hot, "dp", k), plane(k) * 2 * half, axis=0
        )
    x_hidden = jnp.concatenate([ring(of_x(hidden_all, k, 0), "x", k) for k in xs])
    hot_out = back_to_x(dot(x_hidden, hot_down, ((1,), (0,)))).astype(BF)
    hot_outs = jnp.concatenate([hot_out[:half], swap(hot_out[half:])])
    weigh = jnp.concatenate([weigh_mine, weigh_other])

    mixed = dot(combine[0], back, ((1,), (0,)))
    for i in (1, 2):
        mixed = mixed + dot(combine[i], back, ((1,), (0,)))
    for weigh_i in split3(weigh):
        mixed = mixed + dot(weigh_i, hot_outs, ((0,), (0,)))

    mixed = mixed.astype(BF).reshape(n_dp, rows, part)
    mixed_out = jnp.zeros((rows, width), BF)
    for k in ks:
        mixed_out = lax.dynamic_update_slice_in_dim(
            mixed_out, ring(mixed[k], "dp", -k), (me + k) % n_dp * part, axis=1
        )
    context = attend_block(
        after(queries, hidden), draft_keys, draft_values, cache_keys, cache_values, cache_lengths
    )
    return (mixed_out, context)


def solution(mesh):
    chips = Mesh(mesh.devices.reshape(mesh.shape["dp"], 4, -1, 2), ALL)
    in_specs = (
        P(ALL, None),
        P(ALL, None),
        P(ALL, None),
        P(),
        P(PLANE, None, "dp"),
        P(PLANE, None, "dp"),
        P(ALL, None, None),
        P(ALL, None, None),
        P(ALL, None, None),
        P(ALL, None, None),
        P(ALL, None, None),
        P(ALL),
    )
    out_specs = (P(ALL, None), P(ALL, None, None))
    return jax.shard_map(
        per_device, mesh=chips, in_specs=in_specs, out_specs=out_specs, check_vma=False
    )
```

```python
import functools
import math

import jax
import jax.numpy as jnp
from jax import lax
from jax.experimental import pallas as pl
from jax.experimental.pallas import tpu as pltpu
from jax.sharding import Mesh
from jax.sharding import PartitionSpec as P

HEAD_DIM = 128
HOT = 2
CAP = 2
HOT_ROWS = 4
LANES = 128
PLANE = ("x", "z", "core")
ALL = ("dp",) + PLANE
BF = jnp.bfloat16
F32 = jnp.float32


def attend_block(queries, draft_keys, draft_values, cache_keys, cache_values, cache_lengths):
    req_here, drafts, query_width = queries.shape
    context_len = cache_keys.shape[1]
    groups = draft_keys.shape[2] // HEAD_DIM
    per_group = query_width // (groups * HEAD_DIM)
    scaling = 1.0 / math.sqrt(HEAD_DIM)
    query_heads = queries.reshape(req_here, drafts, groups, per_group, HEAD_DIM)
    cache_k = cache_keys.reshape(req_here, context_len, groups, HEAD_DIM)
    cache_v = cache_values.reshape(req_here, context_len, groups, HEAD_DIM)
    draft_k = draft_keys.reshape(req_here, drafts, groups, HEAD_DIM)
    draft_v = draft_values.reshape(req_here, drafts, groups, HEAD_DIM)
    score_cache = (
        jnp.einsum("rigpe,rcge->rgpic", query_heads, cache_k, preferred_element_type=jnp.float32)
        * scaling
    )
    score_draft = (
        jnp.einsum("rigpe,rjge->rgpij", query_heads, draft_k, preferred_element_type=jnp.float32)
        * scaling
    )
    live_cache = jnp.arange(context_len, dtype=jnp.int32)[None, :] < cache_lengths[:, None]
    live_draft = (
        jnp.arange(drafts, dtype=jnp.int32)[None, :] <= jnp.arange(drafts, dtype=jnp.int32)[:, None]
    )
    score_cache = jnp.where(live_cache[:, None, None, None, :], score_cache, -1e30)
    score_draft = jnp.where(live_draft[None, None, None, :, :], score_draft, -1e30)
    highest = jnp.maximum(jnp.max(score_cache, axis=-1), jnp.max(score_draft, axis=-1))
    expo_cache = jnp.exp(score_cache - highest[..., None])
    expo_draft = jnp.exp(score_draft - highest[..., None])
    totals = jnp.sum(expo_cache, axis=-1) + jnp.sum(expo_draft, axis=-1)
    prob_cache = (expo_cache / totals[..., None]).astype(jnp.bfloat16)
    prob_draft = (expo_draft / totals[..., None]).astype(jnp.bfloat16)
    result = jnp.einsum(
        "rgpic,rcge->rigpe", prob_cache, cache_v, preferred_element_type=jnp.float32
    )
    result = result + jnp.einsum(
        "rgpij,rjge->rigpe", prob_draft, draft_v, preferred_element_type=jnp.float32
    )
    return result.astype(jnp.bfloat16).reshape(req_here, drafts, query_width)


def ring(x, axis, k, n=4):
    k = k % n
    return x if k == 0 else lax.ppermute(x, axis, [(i, (i + k) % n) for i in range(n)])


def swap(x):
    return lax.ppermute(x, "core", [(0, 1), (1, 0)])


def after(x, *others):
    return lax.optimization_barrier((x, *others))[0]


def dot(a, b, dims, batch=()):
    return lax.dot_general(a, b, (dims, (batch, batch)), preferred_element_type=F32)


def split3(x):
    hi = lax.reduce_precision(x, 8, 7)
    mid = lax.reduce_precision(x - hi, 8, 7)
    lo = x - hi - mid
    return [v.astype(BF) for v in (hi, mid, lo)]


def pack_copies(gate_ref, down_ref, slot, out_ref, sem):
    n = out_ref.shape[0]
    gate_rows, down_rows = gate_ref.shape[1] // n, down_ref.shape[1] // n
    wide, down_wide = gate_ref.shape[2], down_ref.shape[2]
    pairs = []
    for i in range(n):
        pairs.append(
            (gate_ref.at[slot, pl.ds(i * gate_rows, gate_rows)], out_ref.at[i, pl.ds(0, gate_rows)])
        )
        at = gate_rows
        for column in range(0, down_wide, wide):
            size = min(wide, down_wide - column)
            pairs.append(
                (
                    down_ref.at[slot, pl.ds(i * down_rows, down_rows), pl.ds(column, size)],
                    out_ref.at[i, pl.ds(at, down_rows), pl.ds(0, size)],
                )
            )
            at += down_rows
    return [pltpu.make_async_copy(a, b, sem.at[j]) for j, (a, b) in enumerate(pairs)]


def run_all(copies):
    for copy in copies:
        copy.start()
    for copy in copies:
        copy.wait()


def pack_kernel(slot_ref, gate_ref, down_ref, out_ref, sem):
    run_all(pack_copies(gate_ref, down_ref, slot_ref[0], out_ref, sem))


def hold_kernel(choice_ref, gate_ref, down_ref, theirs_ref, first_ref, out_ref, zeros, sem):
    n = out_ref.shape[0]

    @pl.when(choice_ref[0] == 1)
    def _():
        run_all(pack_copies(gate_ref, down_ref, choice_ref[1], out_ref, sem))

    @pl.when(choice_ref[0] == 2)
    def _():
        run_all(
            [pltpu.make_async_copy(theirs_ref.at[i], out_ref.at[i], sem.at[i]) for i in range(n)]
        )

    @pl.when(choice_ref[0] == 0)
    def _():
        zeros[...] = jnp.zeros_like(zeros)
        run_all([pltpu.make_async_copy(zeros, out_ref.at[i], sem.at[i]) for i in range(n)])


def packed_shape(gate_up, down, n):
    wide = gate_up.shape[2]
    blocks = -(-down.shape[2] // wide)
    return (n, gate_up.shape[1] // n + blocks * down.shape[1] // n, wide), n * (1 + blocks)


def copy_call(kernel, operands, out_shapes, scratch, moved):
    in_hbm = pl.BlockSpec(memory_space=pl.ANY)
    return pl.pallas_call(
        kernel,
        out_shape=out_shapes,
        in_specs=[pl.BlockSpec(memory_space=pltpu.SMEM)] + [in_hbm] * (len(operands) - 1),
        out_specs=jax.tree.map(lambda _: in_hbm, out_shapes),
        scratch_shapes=scratch,
        cost_estimate=pl.CostEstimate(flops=0, bytes_accessed=2 * moved, transcendentals=0),
    )(*operands)


def pack(slot, gate_up, down, n):
    shape, copies = packed_shape(gate_up, down, n)
    out = jax.ShapeDtypeStruct(shape, BF)
    return copy_call(
        pack_kernel, (slot[None], gate_up, down), out, [pltpu.SemaphoreType.DMA((copies,))],
        2 * math.prod(shape),
    )


def hold(choice, slot, gate_up, down, theirs, first):
    shape, copies = packed_shape(gate_up, down, theirs.shape[0])
    out = jax.ShapeDtypeStruct(shape, BF)
    return copy_call(
        hold_kernel, (jnp.stack([choice, slot]), gate_up, down, theirs, first), out,
        [pltpu.VMEM(shape[1:], BF), pltpu.SemaphoreType.DMA((copies,))], 2 * math.prod(shape),
    )


def unpack(piece, gate_rows, down_rows, down_wide):
    blocks = [piece[at : at + down_rows] for at in range(gate_rows, piece.shape[0], down_rows)]
    return piece[:gate_rows], jnp.concatenate(blocks, axis=1)[:, :down_wide]


def cut_kernel(count, at_ref, gate_ref, *refs):
    outs, sem = refs[-1 - count : -1], refs[-1]
    rows = outs[0].shape[1]
    copies = []
    for k, out_ref in enumerate(outs):
        start = pl.multiple_of(at_ref[k] * rows, rows)
        copies.append(
            pltpu.make_async_copy(gate_ref.at[:, pl.ds(start, rows)], out_ref, sem.at[k])
        )
    run_all(copies)


def cut(gate_up, at, n, *others):
    per, width, wide = gate_up.shape
    out = jax.ShapeDtypeStruct((per, width // n, wide), BF)
    return copy_call(
        functools.partial(cut_kernel, at.shape[0]), (at, gate_up, *others), [out] * at.shape[0],
        [pltpu.SemaphoreType.DMA((at.shape[0],))], 2 * at.shape[0] * math.prod(out.shape),
    )


def settle_kernel(x_ref, *refs):
    pass


def settle(x, micros, *others):
    in_hbm = pl.BlockSpec(memory_space=pl.ANY)
    return pl.pallas_call(
        settle_kernel,
        out_shape=jax.ShapeDtypeStruct(x.shape, x.dtype),
        in_specs=[in_hbm] * (1 + len(others)),
        out_specs=in_hbm,
        input_output_aliases={0: 0},
        cost_estimate=pl.CostEstimate(
            flops=micros * 1_000_000_000, bytes_accessed=micros * 3_000_000, transcendentals=0
        ),
    )(x, *others)


def partial_kernel(x_ref, w_ref, out_ref):
    sources, lines, part = x_ref.shape
    per = w_ref.shape[0]
    chunk = lines // per
    x = x_ref[...].reshape(sources * lines, part)
    for s in range(per):
        y = jnp.dot(x, w_ref[s], preferred_element_type=F32).reshape(sources, lines, -1)
        y = y[:, s * chunk : (s + 1) * chunk].reshape(sources * chunk, -1)
        out_ref[pl.ds(s * sources * chunk, sources * chunk), :] = y.astype(out_ref.dtype)


def partial_sums(arrived, weights, dtype):
    sources, lines, part = arrived.shape
    return pl.pallas_call(
        partial_kernel,
        out_shape=jax.ShapeDtypeStruct((sources * lines, weights.shape[2]), dtype),
        compiler_params=pltpu.CompilerParams(vmem_limit_bytes=48 * 2**20),
        cost_estimate=pl.CostEstimate(
            flops=2 * sources * lines * part * weights.shape[2],
            bytes_accessed=2 * (arrived.size + weights.size),
            transcendentals=0,
        ),
    )(arrived, weights)


def place_kernel(picks, info_ref, hot_ref, plane_ref, rows_ref, out_ref, combine_ref, rank_ref):
    info = info_ref[...].astype(F32)
    tokens, slots = info.shape[0], hot_ref.shape[1]
    rows = tokens // 4
    chunk = out_ref.shape[0] // slots
    lane = lax.broadcasted_iota(jnp.int32, (tokens, slots), 1).astype(F32)
    takes = jnp.zeros((tokens, slots), F32)
    weights = [jnp.zeros((tokens, slots), F32) for _ in range(3)]
    for k in range(picks):
        match = lane == info[:, k : k + 1]
        takes = jnp.where(match, 1.0, takes)
        for i in range(3):
            at = (i + 1) * picks + k
            weights[i] = jnp.where(match, info[:, at : at + 1], weights[i])
    early = lax.broadcasted_iota(jnp.int32, (tokens, tokens), 1)
    late = lax.broadcasted_iota(jnp.int32, (tokens, tokens), 0)
    before = late > early
    for k in range(1, 4):
        before = before & ((late >= k * rows) == (early >= k * rows))
    rank = jnp.dot(
        before.astype(BF), takes.astype(BF), preferred_element_type=F32
    )
    rank_ref[...] = jnp.where(takes > 0, rank, -1.0)
    cold = (takes > 0) & (hot_ref[...] == 0)
    code = jnp.where(cold, plane_ref[...] * CAP + rank, -1.0)
    wide = slots * chunk
    slot_at = lax.broadcasted_iota(jnp.int32, (slots, wide), 0)
    column = lax.broadcasted_iota(jnp.int32, (slots, wide), 1)
    spread = (column // chunk == slot_at).astype(BF)
    code = jnp.dot(code.astype(BF), spread, preferred_element_type=F32)
    turn = lax.broadcasted_iota(jnp.int32, (tokens, wide), 1) % chunk
    place = code == turn.astype(F32)
    for i in range(3):
        spread_weight = jnp.dot(weights[i].astype(BF), spread, preferred_element_type=F32)
        combine_ref[i] = jnp.where(place, spread_weight, 0.0).astype(BF)
    out_ref[...] = lax.dot_general(
        place.astype(BF), rows_ref[...], (((0,), (0,)), ((), ())), preferred_element_type=F32
    ).astype(BF)


def place_rows(infos, hot, planes, my_part, picks, chunk):
    tokens, part = my_part.shape
    slots = hot.shape[1]
    return pl.pallas_call(
        functools.partial(place_kernel, picks),
        out_shape=(
            jax.ShapeDtypeStruct((slots * chunk, part), BF),
            jax.ShapeDtypeStruct((3, tokens, slots * chunk), BF),
            jax.ShapeDtypeStruct((tokens, slots), F32),
        ),
        compiler_params=pltpu.CompilerParams(vmem_limit_bytes=32 * 2**20),
        cost_estimate=pl.CostEstimate(
            flops=1_000_000_000, bytes_accessed=4_000_000, transcendentals=0
        ),
    )(infos, hot, planes, my_part)


def per_device(
    tokens,
    route_ids,
    route_weights,
    placement,
    gate_up,
    down,
    queries,
    draft_keys,
    draft_values,
    cache_keys,
    cache_values,
    cache_lengths,
):
    n_dp, n_x = lax.axis_size("dp"), lax.axis_size("x")
    n_expert = lax.axis_size(PLANE)
    me, here = lax.axis_index("dp"), lax.axis_index(PLANE)
    here_x, core = lax.axis_index("x"), lax.axis_index("core")
    rows, picks = route_ids.shape
    slots = placement.shape[0]
    per = gate_up.shape[0]
    width = tokens.shape[1]
    part = width // n_dp
    quarter = gate_up.shape[2] // 2
    chunk = n_dp * CAP
    all_rows = n_dp * rows
    slot_range = jnp.arange(slots, dtype=jnp.int32)
    ks, xs = range(n_dp), range(n_x)

    def plane(k):
        return (me + n_dp - k) % n_dp

    slot_of = jnp.sum(
        jnp.where(route_ids[:, :, None] == slot_range, placement, 0), axis=2
    )
    info = jnp.concatenate([slot_of.astype(BF)] + split3(route_weights), axis=1)
    info = jnp.pad(info, ((0, 0), (0, LANES - info.shape[1])))
    sent = jnp.concatenate([tokens, info], axis=1)
    came = [ring(sent, "dp", k) for k in ks]
    came_tokens = [x[:, :width] for x in came]
    infos = jnp.concatenate([x[:, width:] for x in came], axis=0)
    my_part = jnp.concatenate(
        [lax.dynamic_slice_in_dim(x, me * part, part, axis=1) for x in came_tokens], axis=0
    )

    own = jnp.sum(slot_of[:, :, None] == slot_range, axis=(0, 1))
    hot = own > CAP
    first_hot = jnp.min(jnp.where(hot, slot_range, slots - 1))
    last_hot = jnp.max(jnp.where(hot, slot_range, 0))
    my_hot = jnp.where(core == 0, first_hot, last_hot)
    other_hot = jnp.where(core == 0, last_hot, first_hot)

    owner = my_hot // per

    theirs = swap(pack(other_hot % per, gate_up, down, n_x))
    choice = jnp.where(owner == here, 1, jnp.where(owner == here + 1 - 2 * core, 2, 0))

    others = (me + jnp.arange(1, n_dp, dtype=jnp.int32)) % n_dp
    to_send = cut(gate_up, others, n_dp)
    pieces = [None] + [ring(x, "dp", k) for k, x in zip(ks[1:], to_send)]

    plane_of = (me + n_dp - jnp.arange(all_rows, dtype=jnp.int32) // rows) % n_dp
    planes = plane_of.astype(F32)[:, None]
    my_part = settle(my_part, 1, *to_send)
    outgoing, combine, rank_of = place_rows(
        infos, hot[None, :].astype(jnp.int32), planes, my_part, picks, chunk
    )
    held = hold(choice, my_hot % per, gate_up, down, theirs, outgoing)
    piece = lax.psum_scatter(held, "x", scatter_dimension=0, tiled=False)
    arrived = lax.all_to_all(
        outgoing.reshape(n_expert, per * chunk, part), PLANE, 0, 0, tiled=True
    )

    pieces[0] = cut(gate_up, me[None], n_dp, arrived)[0]
    pieces[2] = settle(pieces[2], 40)
    pieces[3] = settle(pieces[3], 1, piece)
    total = partial_sums(arrived, pieces[0], F32)
    for k in ks[1:]:
        total = total + ring(partial_sums(arrived, pieces[k], BF), "dp", -k).astype(F32)
    hidden = jax.nn.silu(total[:, :quarter]) * total[:, quarter:]
    hidden = jnp.swapaxes(hidden.astype(BF).reshape(per, -1, quarter), 1, 2)
    outs = [0.0] * per
    for k in ks:
        hidden_k = ring(hidden, "dp", k)
        for s in range(per):
            down_piece = lax.dynamic_slice(down, (s, plane(k) * quarter, 0), (1, quarter, part))[0]
            outs[s] = outs[s] + dot(hidden_k[s], down_piece, ((0,), (0,)))
    out = jnp.concatenate([o.astype(BF).reshape(n_expert, chunk, part) for o in outs], axis=1)
    back = lax.all_to_all(out, PLANE, 0, 0, tiled=True).reshape(slots * chunk, part)

    came_slots = infos[:, :picks].astype(jnp.int32)
    came_weights = sum(infos[:, i * picks : (i + 1) * picks].astype(F32) for i in (1, 2, 3))

    def hot_rows_of(slot):
        rank = jnp.sum(jnp.where(slot_range == slot, rank_of, 0.0), axis=1).astype(jnp.int32)
        code = jnp.where(rank >= 0, plane_of * HOT_ROWS + rank, -1)
        find = code[None, :] == jnp.arange(n_dp * HOT_ROWS, dtype=jnp.int32)[:, None]
        weight = jnp.sum(jnp.where(came_slots == slot, came_weights, 0.0), axis=1)
        return find, jnp.where(find, weight, 0.0)

    came_all = jnp.concatenate(came_tokens, axis=0)
    find_mine, weigh_mine = hot_rows_of(my_hot)
    find_other, weigh_other = hot_rows_of(other_hot)
    half = n_dp * HOT_ROWS
    found = dot(jnp.concatenate([find_mine, find_other]).astype(BF), came_all, ((1,), (0,)))
    found = after(found.astype(BF), arrived)
    found = jnp.concatenate([found[:half], swap(found[half:])])

    def of_x(x, k, axis):
        size = x.shape[axis] // n_x
        return lax.dynamic_slice_in_dim(x, (here_x + k) % n_x * size, size, axis=axis)

    def back_to_x(x):
        size = x.shape[0] // n_x
        total = x[:size]
        for k in xs[1:]:
            sent_back = x[k * size : (k + 1) * size].astype(BF)
            total = total + ring(sent_back, "x", -k).astype(F32)
        return total

    x_rows = jnp.concatenate([ring(of_x(found, k, 1), "x", k) for k in xs])
    piece = after(lax.psum(piece, "z"), out)
    hot_gate, hot_down = unpack(piece, width // n_x, down.shape[1] // n_x, part)
    gated = back_to_x(dot(x_rows, hot_gate, ((1,), (0,))))
    hidden_hot = (jax.nn.silu(gated[:, :quarter]) * gated[:, quarter:]).astype(BF)
    hidden_all = jnp.zeros((n_dp * 2 * half, quarter), BF)
    for k in ks:
        hidden_all = lax.dynamic_update_slice_in_dim(
            hidden_all, ring(hidden_hot, "dp", k), plane(k) * 2 * half, axis=0
        )
    x_hidden = jnp.concatenate([ring(of_x(hidden_all, k, 0), "x", k) for k in xs])
    hot_out = back_to_x(dot(x_hidden, hot_down, ((1,), (0,)))).astype(BF)
    hot_outs = jnp.concatenate([hot_out[:half], swap(hot_out[half:])])
    weigh = jnp.concatenate([weigh_mine, weigh_other])

    mixed = dot(combine[0], back, ((1,), (0,)))
    for i in (1, 2):
        mixed = mixed + dot(combine[i], back, ((1,), (0,)))
    for weigh_i in split3(weigh):
        mixed = mixed + dot(weigh_i, hot_outs, ((0,), (0,)))

    mixed = mixed.astype(BF).reshape(n_dp, rows, part)
    mixed_out = jnp.zeros((rows, width), BF)
    for k in ks:
        mixed_out = lax.dynamic_update_slice_in_dim(
            mixed_out, ring(mixed[k], "dp", -k), (me + k) % n_dp * part, axis=1
        )
    late = lax.optimization_barrier(
        (queries, draft_keys, draft_values, cache_keys, cache_values, cache_lengths, hidden)
    )
    context = attend_block(*late[:-1])
    return (mixed_out, context)


def solution(mesh):
    chips = Mesh(mesh.devices.reshape(mesh.shape["dp"], 4, -1, 2), ALL)
    in_specs = (
        P(ALL, None),
        P(ALL, None),
        P(ALL, None),
        P(),
        P(PLANE, None, "dp"),
        P(PLANE, None, "dp"),
        P(ALL, None, None),
        P(ALL, None, None),
        P(ALL, None, None),
        P(ALL, None, None),
        P(ALL, None, None),
        P(ALL),
    )
    out_specs = (P(ALL, None), P(ALL, None, None))
    return jax.shard_map(
        per_device, mesh=chips, in_specs=in_specs, out_specs=out_specs, check_vma=False
    )
```

```python
import functools
import math

import jax
import jax.numpy as jnp
from jax import lax
from jax.experimental import pallas as pl
from jax.experimental.pallas import tpu as pltpu
from jax.sharding import Mesh
from jax.sharding import PartitionSpec as P

HEAD_DIM = 128
HOT = 2
CAP = 2
HOT_ROWS = 4
LANES = 128
PLANE = ("x", "z", "core")
ALL = ("dp",) + PLANE
BF = jnp.bfloat16
F32 = jnp.float32


def attend_block(queries, draft_keys, draft_values, cache_keys, cache_values, cache_lengths):
    req_here, drafts, query_width = queries.shape
    context_len = cache_keys.shape[1]
    groups = draft_keys.shape[2] // HEAD_DIM
    per_group = query_width // (groups * HEAD_DIM)
    scaling = 1.0 / math.sqrt(HEAD_DIM)
    query_heads = queries.reshape(req_here, drafts, groups, per_group, HEAD_DIM)
    cache_k = cache_keys.reshape(req_here, context_len, groups, HEAD_DIM)
    cache_v = cache_values.reshape(req_here, context_len, groups, HEAD_DIM)
    draft_k = draft_keys.reshape(req_here, drafts, groups, HEAD_DIM)
    draft_v = draft_values.reshape(req_here, drafts, groups, HEAD_DIM)
    score_cache = (
        jnp.einsum("rigpe,rcge->rgpic", query_heads, cache_k, preferred_element_type=jnp.float32)
        * scaling
    )
    score_draft = (
        jnp.einsum("rigpe,rjge->rgpij", query_heads, draft_k, preferred_element_type=jnp.float32)
        * scaling
    )
    live_cache = jnp.arange(context_len, dtype=jnp.int32)[None, :] < cache_lengths[:, None]
    live_draft = (
        jnp.arange(drafts, dtype=jnp.int32)[None, :] <= jnp.arange(drafts, dtype=jnp.int32)[:, None]
    )
    score_cache = jnp.where(live_cache[:, None, None, None, :], score_cache, -1e30)
    score_draft = jnp.where(live_draft[None, None, None, :, :], score_draft, -1e30)
    highest = jnp.maximum(jnp.max(score_cache, axis=-1), jnp.max(score_draft, axis=-1))
    expo_cache = jnp.exp(score_cache - highest[..., None])
    expo_draft = jnp.exp(score_draft - highest[..., None])
    totals = jnp.sum(expo_cache, axis=-1) + jnp.sum(expo_draft, axis=-1)
    prob_cache = (expo_cache / totals[..., None]).astype(jnp.bfloat16)
    prob_draft = (expo_draft / totals[..., None]).astype(jnp.bfloat16)
    result = jnp.einsum(
        "rgpic,rcge->rigpe", prob_cache, cache_v, preferred_element_type=jnp.float32
    )
    result = result + jnp.einsum(
        "rgpij,rjge->rigpe", prob_draft, draft_v, preferred_element_type=jnp.float32
    )
    return result.astype(jnp.bfloat16).reshape(req_here, drafts, query_width)


def ring(x, axis, k, n=4):
    k = k % n
    return x if k == 0 else lax.ppermute(x, axis, [(i, (i + k) % n) for i in range(n)])


def swap(x):
    return lax.ppermute(x, "core", [(0, 1), (1, 0)])


def after(x, *others):
    return lax.optimization_barrier((x, *others))[0]


def dot(a, b, dims, batch=()):
    return lax.dot_general(a, b, (dims, (batch, batch)), preferred_element_type=F32)


def split3(x):
    hi = lax.reduce_precision(x, 8, 7)
    mid = lax.reduce_precision(x - hi, 8, 7)
    lo = x - hi - mid
    return [v.astype(BF) for v in (hi, mid, lo)]


def pack_slice(gate_ref, down_ref, slot, i, n, to_ref, sem):
    gate_rows, down_rows = gate_ref.shape[1] // n, down_ref.shape[1] // n
    wide, down_wide = gate_ref.shape[2], down_ref.shape[2]
    pairs = [(gate_ref.at[slot, pl.ds(i * gate_rows, gate_rows)], to_ref.at[pl.ds(0, gate_rows)])]
    at = gate_rows
    for column in range(0, down_wide, wide):
        size = min(wide, down_wide - column)
        pairs.append(
            (
                down_ref.at[slot, pl.ds(i * down_rows, down_rows), pl.ds(column, size)],
                to_ref.at[pl.ds(at, down_rows), pl.ds(0, size)],
            )
        )
        if size < wide:
            to_ref[pl.ds(at, down_rows), pl.ds(size, wide - size)] = jnp.zeros(
                (down_rows, wide - size), BF
            )
        at += down_rows
    return [pltpu.make_async_copy(x, y, sem.at[j]) for j, (x, y) in enumerate(pairs)]


def through(ins, outs):
    for group in ins:
        for copy in group:
            copy.start()
    for group, out in zip(ins, outs):
        for copy in group:
            copy.wait()
        out.start()
    for out in outs:
        out.wait()


def pack_all(gate_ref, down_ref, slot, out_ref, buffer, in_sem, out_sem):
    n = out_ref.shape[0]
    through(
        [pack_slice(gate_ref, down_ref, slot, i, n, buffer.at[i], in_sem.at[i]) for i in range(n)],
        [pltpu.make_async_copy(buffer.at[i], out_ref.at[i], out_sem.at[i]) for i in range(n)],
    )


def pack_kernel(slot_ref, gate_ref, down_ref, out_ref, buffer, in_sem, out_sem):
    pack_all(gate_ref, down_ref, slot_ref[0], out_ref, buffer, in_sem, out_sem)


def hold_kernel(
    choice_ref, gate_ref, down_ref, theirs_ref, first_ref, out_ref, buffer, in_sem, out_sem
):
    n = out_ref.shape[0]

    @pl.when(choice_ref[0] == 1)
    def _():
        pack_all(gate_ref, down_ref, choice_ref[1], out_ref, buffer, in_sem, out_sem)

    @pl.when(choice_ref[0] == 2)
    def _():
        through(
            [
                [pltpu.make_async_copy(theirs_ref.at[i], buffer.at[i], in_sem.at[i, 0])]
                for i in range(n)
            ],
            [pltpu.make_async_copy(buffer.at[i], out_ref.at[i], out_sem.at[i]) for i in range(n)],
        )

    @pl.when(choice_ref[0] == 0)
    def _():
        buffer[0] = jnp.zeros(buffer.shape[1:], BF)
        copies = [pltpu.make_async_copy(buffer.at[0], out_ref.at[i], out_sem.at[i]) for i in range(n)]
        for copy in copies:
            copy.start()
        for copy in copies:
            copy.wait()


def packed_shape(gate_up, down, n):
    wide = gate_up.shape[2]
    blocks = -(-down.shape[2] // wide)
    shape = (n, gate_up.shape[1] // n + blocks * down.shape[1] // n, wide)
    dma = pltpu.SemaphoreType.DMA
    return shape, [pltpu.VMEM(shape, BF), dma((n, 1 + blocks)), dma((n,))]


def copy_call(kernel, operands, out_shapes, scratch, moved):
    in_hbm = pl.BlockSpec(memory_space=pl.ANY)
    return pl.pallas_call(
        kernel,
        out_shape=out_shapes,
        in_specs=[pl.BlockSpec(memory_space=pltpu.SMEM)] + [in_hbm] * (len(operands) - 1),
        out_specs=jax.tree.map(lambda _: in_hbm, out_shapes),
        scratch_shapes=scratch,
        compiler_params=pltpu.CompilerParams(vmem_limit_bytes=16 * 2**20),
        cost_estimate=pl.CostEstimate(flops=0, bytes_accessed=2 * moved, transcendentals=0),
    )(*operands)


def pack(slot, gate_up, down, n):
    shape, scratch = packed_shape(gate_up, down, n)
    out = jax.ShapeDtypeStruct(shape, BF)
    return copy_call(
        pack_kernel, (slot[None], gate_up, down), out, scratch, 2 * math.prod(shape)
    )


def hold(choice, slot, gate_up, down, theirs, first):
    shape, scratch = packed_shape(gate_up, down, theirs.shape[0])
    out = jax.ShapeDtypeStruct(shape, BF)
    return copy_call(
        hold_kernel, (jnp.stack([choice, slot]), gate_up, down, theirs, first), out, scratch,
        2 * math.prod(shape),
    )


def unpack(piece, gate_rows, down_rows, down_wide):
    blocks = [piece[at : at + down_rows] for at in range(gate_rows, piece.shape[0], down_rows)]
    return piece[:gate_rows], jnp.concatenate(blocks, axis=1)[:, :down_wide]


def cut_kernel(count, at_ref, gate_ref, *refs):
    outs, buffer, in_sem, out_sem = refs[-3 - count : -3], refs[-3], refs[-2], refs[-1]
    per, rows = outs[0].shape[:2]
    ins, back = [], []
    for k, out_ref in enumerate(outs):
        start = pl.multiple_of(at_ref[k] * rows, rows)
        for s in range(per):
            block = buffer.at[k, s]
            ins.append(
                [pltpu.make_async_copy(gate_ref.at[s, pl.ds(start, rows)], block, in_sem.at[k, s])]
            )
            back.append(pltpu.make_async_copy(block, out_ref.at[s], out_sem.at[k, s]))
    through(ins, back)


def cut(gate_up, at, n, *others):
    per, width, wide = gate_up.shape
    count = at.shape[0]
    out = jax.ShapeDtypeStruct((per, width // n, wide), BF)
    dma = pltpu.SemaphoreType.DMA
    return copy_call(
        functools.partial(cut_kernel, count), (at, gate_up, *others), [out] * count,
        [pltpu.VMEM((count,) + out.shape, BF), dma((count, per)), dma((count, per))],
        2 * count * math.prod(out.shape),
    )


def settle_kernel(x_ref, *refs):
    pass


def settle(x, micros, *others):
    in_hbm = pl.BlockSpec(memory_space=pl.ANY)
    return pl.pallas_call(
        settle_kernel,
        out_shape=jax.ShapeDtypeStruct(x.shape, x.dtype),
        in_specs=[in_hbm] * (1 + len(others)),
        out_specs=in_hbm,
        input_output_aliases={0: 0},
        cost_estimate=pl.CostEstimate(
            flops=micros * 1_000_000_000, bytes_accessed=micros * 3_000_000, transcendentals=0
        ),
    )(x, *others)


def partial_kernel(x_ref, w_ref, out_ref):
    sources, lines, part = x_ref.shape
    per = w_ref.shape[0]
    chunk = lines // per
    x = x_ref[...].reshape(sources * lines, part)
    for s in range(per):
        y = jnp.dot(x, w_ref[s], preferred_element_type=F32).reshape(sources, lines, -1)
        y = y[:, s * chunk : (s + 1) * chunk].reshape(sources * chunk, -1)
        out_ref[pl.ds(s * sources * chunk, sources * chunk), :] = y.astype(out_ref.dtype)


def partial_sums(arrived, weights, dtype):
    sources, lines, part = arrived.shape
    return pl.pallas_call(
        partial_kernel,
        out_shape=jax.ShapeDtypeStruct((sources * lines, weights.shape[2]), dtype),
        compiler_params=pltpu.CompilerParams(vmem_limit_bytes=48 * 2**20),
        cost_estimate=pl.CostEstimate(
            flops=2 * sources * lines * part * weights.shape[2],
            bytes_accessed=2 * (arrived.size + weights.size),
            transcendentals=0,
        ),
    )(arrived, weights)


def place_kernel(picks, info_ref, hot_ref, plane_ref, rows_ref, out_ref, combine_ref, rank_ref):
    info = info_ref[...].astype(F32)
    tokens, slots = info.shape[0], hot_ref.shape[1]
    rows = tokens // 4
    chunk = out_ref.shape[0] // slots
    lane = lax.broadcasted_iota(jnp.int32, (tokens, slots), 1).astype(F32)
    takes = jnp.zeros((tokens, slots), F32)
    weights = [jnp.zeros((tokens, slots), F32) for _ in range(3)]
    for k in range(picks):
        match = lane == info[:, k : k + 1]
        takes = jnp.where(match, 1.0, takes)
        for i in range(3):
            at = (i + 1) * picks + k
            weights[i] = jnp.where(match, info[:, at : at + 1], weights[i])
    early = lax.broadcasted_iota(jnp.int32, (tokens, tokens), 1)
    late = lax.broadcasted_iota(jnp.int32, (tokens, tokens), 0)
    before = late > early
    for k in range(1, 4):
        before = before & ((late >= k * rows) == (early >= k * rows))
    rank = jnp.dot(
        before.astype(BF), takes.astype(BF), preferred_element_type=F32
    )
    rank_ref[...] = jnp.where(takes > 0, rank, -1.0)
    cold = (takes > 0) & (hot_ref[...] == 0)
    code = jnp.where(cold, plane_ref[...] * CAP + rank, -1.0)
    wide = slots * chunk
    slot_at = lax.broadcasted_iota(jnp.int32, (slots, wide), 0)
    column = lax.broadcasted_iota(jnp.int32, (slots, wide), 1)
    spread = (column // chunk == slot_at).astype(BF)
    code = jnp.dot(code.astype(BF), spread, preferred_element_type=F32)
    turn = lax.broadcasted_iota(jnp.int32, (tokens, wide), 1) % chunk
    place = code == turn.astype(F32)
    for i in range(3):
        spread_weight = jnp.dot(weights[i].astype(BF), spread, preferred_element_type=F32)
        combine_ref[i] = jnp.where(place, spread_weight, 0.0).astype(BF)
    out_ref[...] = lax.dot_general(
        place.astype(BF), rows_ref[...], (((0,), (0,)), ((), ())), preferred_element_type=F32
    ).astype(BF)


def place_rows(infos, hot, planes, my_part, picks, chunk):
    tokens, part = my_part.shape
    slots = hot.shape[1]
    return pl.pallas_call(
        functools.partial(place_kernel, picks),
        out_shape=(
            jax.ShapeDtypeStruct((slots * chunk, part), BF),
            jax.ShapeDtypeStruct((3, tokens, slots * chunk), BF),
            jax.ShapeDtypeStruct((tokens, slots), F32),
        ),
        compiler_params=pltpu.CompilerParams(vmem_limit_bytes=32 * 2**20),
        cost_estimate=pl.CostEstimate(
            flops=1_000_000_000, bytes_accessed=4_000_000, transcendentals=0
        ),
    )(infos, hot, planes, my_part)


def per_device(
    tokens,
    route_ids,
    route_weights,
    placement,
    gate_up,
    down,
    queries,
    draft_keys,
    draft_values,
    cache_keys,
    cache_values,
    cache_lengths,
):
    n_dp, n_x = lax.axis_size("dp"), lax.axis_size("x")
    n_expert = lax.axis_size(PLANE)
    me, here = lax.axis_index("dp"), lax.axis_index(PLANE)
    here_x, core = lax.axis_index("x"), lax.axis_index("core")
    rows, picks = route_ids.shape
    slots = placement.shape[0]
    per = gate_up.shape[0]
    width = tokens.shape[1]
    part = width // n_dp
    quarter = gate_up.shape[2] // 2
    chunk = n_dp * CAP
    all_rows = n_dp * rows
    slot_range = jnp.arange(slots, dtype=jnp.int32)
    ks, xs = range(n_dp), range(n_x)

    def plane(k):
        return (me + n_dp - k) % n_dp

    slot_of = jnp.sum(
        jnp.where(route_ids[:, :, None] == slot_range, placement, 0), axis=2
    )
    info = jnp.concatenate([slot_of.astype(BF)] + split3(route_weights), axis=1)
    info = jnp.pad(info, ((0, 0), (0, LANES - info.shape[1])))
    sent = jnp.concatenate([tokens, info], axis=1)
    came = [ring(sent, "dp", k) for k in ks]
    came_tokens = [x[:, :width] for x in came]
    infos = jnp.concatenate([x[:, width:] for x in came], axis=0)
    my_part = jnp.concatenate(
        [lax.dynamic_slice_in_dim(x, me * part, part, axis=1) for x in came_tokens], axis=0
    )

    own = jnp.sum(slot_of[:, :, None] == slot_range, axis=(0, 1))
    hot = own > CAP
    first_hot = jnp.min(jnp.where(hot, slot_range, slots - 1))
    last_hot = jnp.max(jnp.where(hot, slot_range, 0))
    my_hot = jnp.where(core == 0, first_hot, last_hot)
    other_hot = jnp.where(core == 0, last_hot, first_hot)

    owner = my_hot // per

    theirs = swap(pack(other_hot % per, gate_up, down, n_x))
    choice = jnp.where(owner == here, 1, jnp.where(owner == here + 1 - 2 * core, 2, 0))

    others = (me + jnp.arange(1, n_dp, dtype=jnp.int32)) % n_dp
    to_send = cut(gate_up, others, n_dp)
    pieces = [None] + [ring(x, "dp", k) for k, x in zip(ks[1:], to_send)]

    plane_of = (me + n_dp - jnp.arange(all_rows, dtype=jnp.int32) // rows) % n_dp
    planes = plane_of.astype(F32)[:, None]
    my_part = settle(my_part, 1, *to_send)
    outgoing, combine, rank_of = place_rows(
        infos, hot[None, :].astype(jnp.int32), planes, my_part, picks, chunk
    )
    held = hold(choice, my_hot % per, gate_up, down, theirs, outgoing)
    piece = lax.psum_scatter(held, "x", scatter_dimension=0, tiled=False)
    arrived = lax.all_to_all(
        outgoing.reshape(n_expert, per * chunk, part), PLANE, 0, 0, tiled=True
    )

    pieces[0] = cut(gate_up, me[None], n_dp, arrived)[0]
    pieces[2] = settle(pieces[2], 40)
    pieces[3] = settle(pieces[3], 1, piece)
    total = partial_sums(arrived, pieces[0], F32)
    for k in ks[1:]:
        total = total + ring(partial_sums(arrived, pieces[k], BF), "dp", -k).astype(F32)
    hidden = jax.nn.silu(total[:, :quarter]) * total[:, quarter:]
    hidden = jnp.swapaxes(hidden.astype(BF).reshape(per, -1, quarter), 1, 2)
    outs = [0.0] * per
    for k in ks:
        hidden_k = ring(hidden, "dp", k)
        for s in range(per):
            down_piece = lax.dynamic_slice(down, (s, plane(k) * quarter, 0), (1, quarter, part))[0]
            outs[s] = outs[s] + dot(hidden_k[s], down_piece, ((0,), (0,)))
    out = jnp.concatenate([o.astype(BF).reshape(n_expert, chunk, part) for o in outs], axis=1)
    back = lax.all_to_all(out, PLANE, 0, 0, tiled=True).reshape(slots * chunk, part)

    came_slots = infos[:, :picks].astype(jnp.int32)
    came_weights = sum(infos[:, i * picks : (i + 1) * picks].astype(F32) for i in (1, 2, 3))

    def hot_rows_of(slot):
        rank = jnp.sum(jnp.where(slot_range == slot, rank_of, 0.0), axis=1).astype(jnp.int32)
        code = jnp.where(rank >= 0, plane_of * HOT_ROWS + rank, -1)
        find = code[None, :] == jnp.arange(n_dp * HOT_ROWS, dtype=jnp.int32)[:, None]
        weight = jnp.sum(jnp.where(came_slots == slot, came_weights, 0.0), axis=1)
        return find, jnp.where(find, weight, 0.0)

    came_all = jnp.concatenate(came_tokens, axis=0)
    find_mine, weigh_mine = hot_rows_of(my_hot)
    find_other, weigh_other = hot_rows_of(other_hot)
    half = n_dp * HOT_ROWS
    found = dot(jnp.concatenate([find_mine, find_other]).astype(BF), came_all, ((1,), (0,)))
    found = after(found.astype(BF), arrived)
    found = jnp.concatenate([found[:half], swap(found[half:])])

    def of_x(x, k, axis):
        size = x.shape[axis] // n_x
        return lax.dynamic_slice_in_dim(x, (here_x + k) % n_x * size, size, axis=axis)

    def back_to_x(x):
        size = x.shape[0] // n_x
        total = x[:size]
        for k in xs[1:]:
            sent_back = x[k * size : (k + 1) * size].astype(BF)
            total = total + ring(sent_back, "x", -k).astype(F32)
        return total

    x_rows = jnp.concatenate([ring(of_x(found, k, 1), "x", k) for k in xs])
    piece = after(lax.psum(piece, "z"), out)
    hot_gate, hot_down = unpack(piece, width // n_x, down.shape[1] // n_x, part)
    gated = back_to_x(dot(x_rows, hot_gate, ((1,), (0,))))
    hidden_hot = (jax.nn.silu(gated[:, :quarter]) * gated[:, quarter:]).astype(BF)
    hidden_all = jnp.zeros((n_dp * 2 * half, quarter), BF)
    for k in ks:
        hidden_all = lax.dynamic_update_slice_in_dim(
            hidden_all, ring(hidden_hot, "dp", k), plane(k) * 2 * half, axis=0
        )
    x_hidden = jnp.concatenate([ring(of_x(hidden_all, k, 0), "x", k) for k in xs])
    hot_out = back_to_x(dot(x_hidden, hot_down, ((1,), (0,)))).astype(BF)
    hot_outs = jnp.concatenate([hot_out[:half], swap(hot_out[half:])])
    weigh = jnp.concatenate([weigh_mine, weigh_other])

    mixed = dot(combine[0], back, ((1,), (0,)))
    for i in (1, 2):
        mixed = mixed + dot(combine[i], back, ((1,), (0,)))
    for weigh_i in split3(weigh):
        mixed = mixed + dot(weigh_i, hot_outs, ((0,), (0,)))

    mixed = mixed.astype(BF).reshape(n_dp, rows, part)
    mixed_out = jnp.zeros((rows, width), BF)
    for k in ks:
        mixed_out = lax.dynamic_update_slice_in_dim(
            mixed_out, ring(mixed[k], "dp", -k), (me + k) % n_dp * part, axis=1
        )
    late = lax.optimization_barrier(
        (queries, draft_keys, draft_values, cache_keys, cache_values, cache_lengths, hidden)
    )
    context = attend_block(*late[:-1])
    return (mixed_out, context)


def solution(mesh):
    chips = Mesh(mesh.devices.reshape(mesh.shape["dp"], 4, -1, 2), ALL)
    in_specs = (
        P(ALL, None),
        P(ALL, None),
        P(ALL, None),
        P(),
        P(PLANE, None, "dp"),
        P(PLANE, None, "dp"),
        P(ALL, None, None),
        P(ALL, None, None),
        P(ALL, None, None),
        P(ALL, None, None),
        P(ALL, None, None),
        P(ALL),
    )
    out_specs = (P(ALL, None), P(ALL, None, None))
    return jax.shard_map(
        per_device, mesh=chips, in_specs=in_specs, out_specs=out_specs, check_vma=False
    )
```

```python
import functools
import math

import jax
import jax.numpy as jnp
from jax import lax
from jax.experimental import pallas as pl
from jax.experimental.pallas import tpu as pltpu
from jax.sharding import Mesh
from jax.sharding import PartitionSpec as P

HEAD_DIM = 128
HOT = 2
CAP = 2
HOT_ROWS = 4
LANES = 128
PLANE = ("x", "z", "core")
ALL = ("dp",) + PLANE
BF = jnp.bfloat16
F32 = jnp.float32


def attend_block(queries, draft_keys, draft_values, cache_keys, cache_values, cache_lengths):
    req_here, drafts, query_width = queries.shape
    context_len = cache_keys.shape[1]
    groups = draft_keys.shape[2] // HEAD_DIM
    per_group = query_width // (groups * HEAD_DIM)
    scaling = 1.0 / math.sqrt(HEAD_DIM)
    query_heads = queries.reshape(req_here, drafts, groups, per_group, HEAD_DIM)
    cache_k = cache_keys.reshape(req_here, context_len, groups, HEAD_DIM)
    cache_v = cache_values.reshape(req_here, context_len, groups, HEAD_DIM)
    draft_k = draft_keys.reshape(req_here, drafts, groups, HEAD_DIM)
    draft_v = draft_values.reshape(req_here, drafts, groups, HEAD_DIM)
    score_cache = (
        jnp.einsum("rigpe,rcge->rgpic", query_heads, cache_k, preferred_element_type=jnp.float32)
        * scaling
    )
    score_draft = (
        jnp.einsum("rigpe,rjge->rgpij", query_heads, draft_k, preferred_element_type=jnp.float32)
        * scaling
    )
    live_cache = jnp.arange(context_len, dtype=jnp.int32)[None, :] < cache_lengths[:, None]
    live_draft = (
        jnp.arange(drafts, dtype=jnp.int32)[None, :] <= jnp.arange(drafts, dtype=jnp.int32)[:, None]
    )
    score_cache = jnp.where(live_cache[:, None, None, None, :], score_cache, -1e30)
    score_draft = jnp.where(live_draft[None, None, None, :, :], score_draft, -1e30)
    highest = jnp.maximum(jnp.max(score_cache, axis=-1), jnp.max(score_draft, axis=-1))
    expo_cache = jnp.exp(score_cache - highest[..., None])
    expo_draft = jnp.exp(score_draft - highest[..., None])
    totals = jnp.sum(expo_cache, axis=-1) + jnp.sum(expo_draft, axis=-1)
    prob_cache = (expo_cache / totals[..., None]).astype(jnp.bfloat16)
    prob_draft = (expo_draft / totals[..., None]).astype(jnp.bfloat16)
    result = jnp.einsum(
        "rgpic,rcge->rigpe", prob_cache, cache_v, preferred_element_type=jnp.float32
    )
    result = result + jnp.einsum(
        "rgpij,rjge->rigpe", prob_draft, draft_v, preferred_element_type=jnp.float32
    )
    return result.astype(jnp.bfloat16).reshape(req_here, drafts, query_width)


def ring(x, axis, k, n=4):
    k = k % n
    return x if k == 0 else lax.ppermute(x, axis, [(i, (i + k) % n) for i in range(n)])


def swap(x):
    return lax.ppermute(x, "core", [(0, 1), (1, 0)])


def after(x, *others):
    return lax.optimization_barrier((x, *others))[0]


def dot(a, b, dims, batch=()):
    return lax.dot_general(a, b, (dims, (batch, batch)), preferred_element_type=F32)


def split3(x):
    hi = lax.reduce_precision(x, 8, 7)
    mid = lax.reduce_precision(x - hi, 8, 7)
    lo = x - hi - mid
    return [v.astype(BF) for v in (hi, mid, lo)]


def pack_slice(gate_ref, down_ref, slot, i, n, to_ref, sem):
    gate_rows, down_rows = gate_ref.shape[1] // n, down_ref.shape[1] // n
    wide, down_wide = gate_ref.shape[2], down_ref.shape[2]
    pairs = [(gate_ref.at[slot, pl.ds(i * gate_rows, gate_rows)], to_ref.at[pl.ds(0, gate_rows)])]
    at = gate_rows
    for column in range(0, down_wide, wide):
        size = min(wide, down_wide - column)
        pairs.append(
            (
                down_ref.at[slot, pl.ds(i * down_rows, down_rows), pl.ds(column, size)],
                to_ref.at[pl.ds(at, down_rows), pl.ds(0, size)],
            )
        )
        if size < wide:
            to_ref[pl.ds(at, down_rows), pl.ds(size, wide - size)] = jnp.zeros(
                (down_rows, wide - size), BF
            )
        at += down_rows
    return [pltpu.make_async_copy(x, y, sem.at[j]) for j, (x, y) in enumerate(pairs)]


def through(ins, outs):
    for group in ins:
        for copy in group:
            copy.start()
    for group, out in zip(ins, outs):
        for copy in group:
            copy.wait()
        out.start()
    for out in outs:
        out.wait()


def pack_all(gate_ref, down_ref, slot, out_ref, buffer, in_sem, out_sem):
    n = out_ref.shape[0]
    through(
        [pack_slice(gate_ref, down_ref, slot, i, n, buffer.at[i], in_sem.at[i]) for i in range(n)],
        [pltpu.make_async_copy(buffer.at[i], out_ref.at[i], out_sem.at[i]) for i in range(n)],
    )


def pack_kernel(slot_ref, gate_ref, down_ref, out_ref, buffer, in_sem, out_sem):
    pack_all(gate_ref, down_ref, slot_ref[0], out_ref, buffer, in_sem, out_sem)


def hold_kernel(
    choice_ref, gate_ref, down_ref, theirs_ref, first_ref, out_ref, buffer, in_sem, out_sem
):
    n = out_ref.shape[0]

    @pl.when(choice_ref[0] == 1)
    def _():
        pack_all(gate_ref, down_ref, choice_ref[1], out_ref, buffer, in_sem, out_sem)

    @pl.when(choice_ref[0] == 2)
    def _():
        through(
            [
                [pltpu.make_async_copy(theirs_ref.at[i], buffer.at[i], in_sem.at[i, 0])]
                for i in range(n)
            ],
            [pltpu.make_async_copy(buffer.at[i], out_ref.at[i], out_sem.at[i]) for i in range(n)],
        )

    @pl.when(choice_ref[0] == 0)
    def _():
        buffer[0] = jnp.zeros(buffer.shape[1:], BF)
        copies = [pltpu.make_async_copy(buffer.at[0], out_ref.at[i], out_sem.at[i]) for i in range(n)]
        for copy in copies:
            copy.start()
        for copy in copies:
            copy.wait()


def packed_shape(gate_up, down, n):
    wide = gate_up.shape[2]
    blocks = -(-down.shape[2] // wide)
    shape = (n, gate_up.shape[1] // n + blocks * down.shape[1] // n, wide)
    dma = pltpu.SemaphoreType.DMA
    return shape, [pltpu.VMEM(shape, BF), dma((n, 1 + blocks)), dma((n,))]


def copy_call(kernel, operands, out_shapes, scratch, moved):
    in_hbm = pl.BlockSpec(memory_space=pl.ANY)
    return pl.pallas_call(
        kernel,
        out_shape=out_shapes,
        in_specs=[pl.BlockSpec(memory_space=pltpu.SMEM)] + [in_hbm] * (len(operands) - 1),
        out_specs=jax.tree.map(lambda _: in_hbm, out_shapes),
        scratch_shapes=scratch,
        cost_estimate=pl.CostEstimate(flops=0, bytes_accessed=2 * moved, transcendentals=0),
    )(*operands)


def pack(slot, gate_up, down, n):
    shape, scratch = packed_shape(gate_up, down, n)
    out = jax.ShapeDtypeStruct(shape, BF)
    return copy_call(
        pack_kernel, (slot[None], gate_up, down), out, scratch, 2 * math.prod(shape)
    )


def hold(choice, slot, gate_up, down, theirs, first):
    shape, scratch = packed_shape(gate_up, down, theirs.shape[0])
    out = jax.ShapeDtypeStruct(shape, BF)
    return copy_call(
        hold_kernel, (jnp.stack([choice, slot]), gate_up, down, theirs, first), out, scratch,
        2 * math.prod(shape),
    )


def unpack(piece, gate_rows, down_rows, down_wide):
    blocks = [piece[at : at + down_rows] for at in range(gate_rows, piece.shape[0], down_rows)]
    return piece[:gate_rows], jnp.concatenate(blocks, axis=1)[:, :down_wide]


def cut_kernel(count, at_ref, gate_ref, *refs):
    outs, buffer, in_sem, out_sem = refs[-3 - count : -3], refs[-3], refs[-2], refs[-1]
    per, rows = outs[0].shape[:2]
    ins, back = [], []
    for k, out_ref in enumerate(outs):
        start = pl.multiple_of(at_ref[k] * rows, rows)
        for s in range(per):
            block = buffer.at[k, s]
            ins.append(
                [pltpu.make_async_copy(gate_ref.at[s, pl.ds(start, rows)], block, in_sem.at[k, s])]
            )
            back.append(pltpu.make_async_copy(block, out_ref.at[s], out_sem.at[k, s]))
    through(ins, back)


def cut(gate_up, at, n, *others):
    per, width, wide = gate_up.shape
    count = at.shape[0]
    out = jax.ShapeDtypeStruct((per, width // n, wide), BF)
    dma = pltpu.SemaphoreType.DMA
    return copy_call(
        functools.partial(cut_kernel, count), (at, gate_up, *others), [out] * count,
        [pltpu.VMEM((count,) + out.shape, BF), dma((count, per)), dma((count, per))],
        2 * count * math.prod(out.shape),
    )


def settle_kernel(x_ref, *refs):
    pass


def settle(x, micros, *others):
    in_hbm = pl.BlockSpec(memory_space=pl.ANY)
    return pl.pallas_call(
        settle_kernel,
        out_shape=jax.ShapeDtypeStruct(x.shape, x.dtype),
        in_specs=[in_hbm] * (1 + len(others)),
        out_specs=in_hbm,
        input_output_aliases={0: 0},
        cost_estimate=pl.CostEstimate(
            flops=micros * 1_000_000_000, bytes_accessed=micros * 3_000_000, transcendentals=0
        ),
    )(x, *others)


def partial_kernel(x_ref, w_ref, out_ref):
    sources, lines, part = x_ref.shape
    per = w_ref.shape[0]
    chunk = lines // per
    x = x_ref[...].reshape(sources * lines, part)
    for s in range(per):
        y = jnp.dot(x, w_ref[s], preferred_element_type=F32).reshape(sources, lines, -1)
        y = y[:, s * chunk : (s + 1) * chunk].reshape(sources * chunk, -1)
        out_ref[pl.ds(s * sources * chunk, sources * chunk), :] = y.astype(out_ref.dtype)


def partial_sums(arrived, weights, dtype):
    sources, lines, part = arrived.shape
    return pl.pallas_call(
        partial_kernel,
        out_shape=jax.ShapeDtypeStruct((sources * lines, weights.shape[2]), dtype),
        compiler_params=pltpu.CompilerParams(vmem_limit_bytes=48 * 2**20),
        cost_estimate=pl.CostEstimate(
            flops=2 * sources * lines * part * weights.shape[2],
            bytes_accessed=2 * (arrived.size + weights.size),
            transcendentals=0,
        ),
    )(arrived, weights)


def place_kernel(picks, info_ref, hot_ref, plane_ref, rows_ref, out_ref, combine_ref, rank_ref):
    info = info_ref[...].astype(F32)
    tokens, slots = info.shape[0], hot_ref.shape[1]
    rows = tokens // 4
    chunk = out_ref.shape[0] // slots
    lane = lax.broadcasted_iota(jnp.int32, (tokens, slots), 1).astype(F32)
    takes = jnp.zeros((tokens, slots), F32)
    weights = [jnp.zeros((tokens, slots), F32) for _ in range(3)]
    for k in range(picks):
        match = lane == info[:, k : k + 1]
        takes = jnp.where(match, 1.0, takes)
        for i in range(3):
            at = (i + 1) * picks + k
            weights[i] = jnp.where(match, info[:, at : at + 1], weights[i])
    early = lax.broadcasted_iota(jnp.int32, (tokens, tokens), 1)
    late = lax.broadcasted_iota(jnp.int32, (tokens, tokens), 0)
    before = late > early
    for k in range(1, 4):
        before = before & ((late >= k * rows) == (early >= k * rows))
    rank = jnp.dot(
        before.astype(BF), takes.astype(BF), preferred_element_type=F32
    )
    rank_ref[...] = jnp.where(takes > 0, rank, -1.0)
    cold = (takes > 0) & (hot_ref[...] == 0)
    code = jnp.where(cold, plane_ref[...] * CAP + rank, -1.0)
    wide = slots * chunk
    slot_at = lax.broadcasted_iota(jnp.int32, (slots, wide), 0)
    column = lax.broadcasted_iota(jnp.int32, (slots, wide), 1)
    spread = (column // chunk == slot_at).astype(BF)
    code = jnp.dot(code.astype(BF), spread, preferred_element_type=F32)
    turn = lax.broadcasted_iota(jnp.int32, (tokens, wide), 1) % chunk
    place = code == turn.astype(F32)
    for i in range(3):
        spread_weight = jnp.dot(weights[i].astype(BF), spread, preferred_element_type=F32)
        combine_ref[i] = jnp.where(place, spread_weight, 0.0).astype(BF)
    out_ref[...] = lax.dot_general(
        place.astype(BF), rows_ref[...], (((0,), (0,)), ((), ())), preferred_element_type=F32
    ).astype(BF)


def place_rows(infos, hot, planes, my_part, picks, chunk):
    tokens, part = my_part.shape
    slots = hot.shape[1]
    return pl.pallas_call(
        functools.partial(place_kernel, picks),
        out_shape=(
            jax.ShapeDtypeStruct((slots * chunk, part), BF),
            jax.ShapeDtypeStruct((3, tokens, slots * chunk), BF),
            jax.ShapeDtypeStruct((tokens, slots), F32),
        ),
        compiler_params=pltpu.CompilerParams(vmem_limit_bytes=32 * 2**20),
        cost_estimate=pl.CostEstimate(
            flops=1_000_000_000, bytes_accessed=4_000_000, transcendentals=0
        ),
    )(infos, hot, planes, my_part)


def per_device(
    tokens,
    route_ids,
    route_weights,
    placement,
    gate_up,
    down,
    queries,
    draft_keys,
    draft_values,
    cache_keys,
    cache_values,
    cache_lengths,
):
    n_dp, n_x = lax.axis_size("dp"), lax.axis_size("x")
    n_expert = lax.axis_size(PLANE)
    me, here = lax.axis_index("dp"), lax.axis_index(PLANE)
    here_x, core = lax.axis_index("x"), lax.axis_index("core")
    rows, picks = route_ids.shape
    slots = placement.shape[0]
    per = gate_up.shape[0]
    width = tokens.shape[1]
    part = width // n_dp
    quarter = gate_up.shape[2] // 2
    chunk = n_dp * CAP
    all_rows = n_dp * rows
    slot_range = jnp.arange(slots, dtype=jnp.int32)
    ks, xs = range(n_dp), range(n_x)

    def plane(k):
        return (me + n_dp - k) % n_dp

    slot_of = jnp.sum(
        jnp.where(route_ids[:, :, None] == slot_range, placement, 0), axis=2
    )
    info = jnp.concatenate([slot_of.astype(BF)] + split3(route_weights), axis=1)
    info = jnp.pad(info, ((0, 0), (0, LANES - info.shape[1])))
    sent = jnp.concatenate([tokens, info], axis=1)
    came = [ring(sent, "dp", k) for k in ks]
    came_tokens = [x[:, :width] for x in came]
    infos = jnp.concatenate([x[:, width:] for x in came], axis=0)
    my_part = jnp.concatenate(
        [lax.dynamic_slice_in_dim(x, me * part, part, axis=1) for x in came_tokens], axis=0
    )

    own = jnp.sum(slot_of[:, :, None] == slot_range, axis=(0, 1))
    hot = own > CAP
    first_hot = jnp.min(jnp.where(hot, slot_range, slots - 1))
    last_hot = jnp.max(jnp.where(hot, slot_range, 0))
    my_hot = jnp.where(core == 0, first_hot, last_hot)
    other_hot = jnp.where(core == 0, last_hot, first_hot)

    owner = my_hot // per

    theirs = swap(pack(other_hot % per, gate_up, down, n_x))
    choice = jnp.where(owner == here, 1, jnp.where(owner == here + 1 - 2 * core, 2, 0))

    others = (me + jnp.arange(1, n_dp, dtype=jnp.int32)) % n_dp
    to_send = cut(gate_up, others, n_dp)
    pieces = [None] + [ring(x, "dp", k) for k, x in zip(ks[1:], to_send)]

    plane_of = (me + n_dp - jnp.arange(all_rows, dtype=jnp.int32) // rows) % n_dp
    planes = plane_of.astype(F32)[:, None]
    my_part = settle(my_part, 1, *to_send)
    outgoing, combine, rank_of = place_rows(
        infos, hot[None, :].astype(jnp.int32), planes, my_part, picks, chunk
    )
    held = hold(choice, my_hot % per, gate_up, down, theirs, outgoing)
    piece = lax.psum_scatter(held, "x", scatter_dimension=0, tiled=False)
    arrived = lax.all_to_all(
        outgoing.reshape(n_expert, per * chunk, part), PLANE, 0, 0, tiled=True
    )

    pieces[0] = cut(gate_up, me[None], n_dp, to_send[0])[0]
    pieces[2] = settle(pieces[2], 40)
    total = partial_sums(arrived, pieces[0], F32)
    pieces[3] = settle(pieces[3], 1, piece, total)
    for k in ks[1:]:
        total = total + ring(partial_sums(arrived, pieces[k], BF), "dp", -k).astype(F32)
    hidden = jax.nn.silu(total[:, :quarter]) * total[:, quarter:]
    hidden = jnp.swapaxes(hidden.astype(BF).reshape(per, -1, quarter), 1, 2)
    outs = [0.0] * per
    for k in ks:
        hidden_k = ring(hidden, "dp", k)
        for s in range(per):
            down_piece = lax.dynamic_slice(down, (s, plane(k) * quarter, 0), (1, quarter, part))[0]
            outs[s] = outs[s] + dot(hidden_k[s], down_piece, ((0,), (0,)))
    out = jnp.concatenate([o.astype(BF).reshape(n_expert, chunk, part) for o in outs], axis=1)
    back = lax.all_to_all(out, PLANE, 0, 0, tiled=True).reshape(slots * chunk, part)

    came_slots = infos[:, :picks].astype(jnp.int32)
    came_weights = sum(infos[:, i * picks : (i + 1) * picks].astype(F32) for i in (1, 2, 3))

    def hot_rows_of(slot):
        rank = jnp.sum(jnp.where(slot_range == slot, rank_of, 0.0), axis=1).astype(jnp.int32)
        code = jnp.where(rank >= 0, plane_of * HOT_ROWS + rank, -1)
        find = code[None, :] == jnp.arange(n_dp * HOT_ROWS, dtype=jnp.int32)[:, None]
        weight = jnp.sum(jnp.where(came_slots == slot, came_weights, 0.0), axis=1)
        return find, jnp.where(find, weight, 0.0)

    came_all = jnp.concatenate(came_tokens, axis=0)
    find_mine, weigh_mine = hot_rows_of(my_hot)
    find_other, weigh_other = hot_rows_of(other_hot)
    half = n_dp * HOT_ROWS
    found = dot(jnp.concatenate([find_mine, find_other]).astype(BF), came_all, ((1,), (0,)))
    found = after(found.astype(BF), arrived)
    found = jnp.concatenate([found[:half], swap(found[half:])])

    def of_x(x, k, axis):
        size = x.shape[axis] // n_x
        return lax.dynamic_slice_in_dim(x, (here_x + k) % n_x * size, size, axis=axis)

    def back_to_x(x):
        size = x.shape[0] // n_x
        total = x[:size]
        for k in xs[1:]:
            sent_back = x[k * size : (k + 1) * size].astype(BF)
            total = total + ring(sent_back, "x", -k).astype(F32)
        return total

    x_rows = jnp.concatenate([ring(of_x(found, k, 1), "x", k) for k in xs])
    piece = after(lax.psum(piece, "z"), out)
    hot_gate, hot_down = unpack(piece, width // n_x, down.shape[1] // n_x, part)
    gated = back_to_x(dot(x_rows, hot_gate, ((1,), (0,))))
    hidden_hot = (jax.nn.silu(gated[:, :quarter]) * gated[:, quarter:]).astype(BF)
    hidden_all = jnp.zeros((n_dp * 2 * half, quarter), BF)
    for k in ks:
        hidden_all = lax.dynamic_update_slice_in_dim(
            hidden_all, ring(hidden_hot, "dp", k), plane(k) * 2 * half, axis=0
        )
    x_hidden = jnp.concatenate([ring(of_x(hidden_all, k, 0), "x", k) for k in xs])
    hot_out = back_to_x(dot(x_hidden, hot_down, ((1,), (0,)))).astype(BF)
    hot_outs = jnp.concatenate([hot_out[:half], swap(hot_out[half:])])
    weigh = jnp.concatenate([weigh_mine, weigh_other])

    mixed = dot(combine[0], back, ((1,), (0,)))
    for i in (1, 2):
        mixed = mixed + dot(combine[i], back, ((1,), (0,)))
    for weigh_i in split3(weigh):
        mixed = mixed + dot(weigh_i, hot_outs, ((0,), (0,)))

    mixed = mixed.astype(BF).reshape(n_dp, rows, part)
    mixed_out = jnp.zeros((rows, width), BF)
    for k in ks:
        mixed_out = lax.dynamic_update_slice_in_dim(
            mixed_out, ring(mixed[k], "dp", -k), (me + k) % n_dp * part, axis=1
        )
    late = lax.optimization_barrier(
        (queries, draft_keys, draft_values, cache_keys, cache_values, cache_lengths, hidden)
    )
    context = attend_block(*late[:-1])
    return (mixed_out, context)


def solution(mesh):
    chips = Mesh(mesh.devices.reshape(mesh.shape["dp"], 4, -1, 2), ALL)
    in_specs = (
        P(ALL, None),
        P(ALL, None),
        P(ALL, None),
        P(),
        P(PLANE, None, "dp"),
        P(PLANE, None, "dp"),
        P(ALL, None, None),
        P(ALL, None, None),
        P(ALL, None, None),
        P(ALL, None, None),
        P(ALL, None, None),
        P(ALL),
    )
    out_specs = (P(ALL, None), P(ALL, None, None))
    return jax.shard_map(
        per_device, mesh=chips, in_specs=in_specs, out_specs=out_specs, check_vma=False
    )
```

```python
import functools
import math

import jax
import jax.numpy as jnp
from jax import lax
from jax.experimental import pallas as pl
from jax.experimental.pallas import tpu as pltpu
from jax.sharding import Mesh
from jax.sharding import PartitionSpec as P

HEAD_DIM = 128
HOT = 2
CAP = 2
HOT_ROWS = 4
LANES = 128
PLANE = ("x", "z", "core")
ALL = ("dp",) + PLANE
BF = jnp.bfloat16
F32 = jnp.float32


def attend_block(queries, draft_keys, draft_values, cache_keys, cache_values, cache_lengths):
    req_here, drafts, query_width = queries.shape
    context_len = cache_keys.shape[1]
    groups = draft_keys.shape[2] // HEAD_DIM
    per_group = query_width // (groups * HEAD_DIM)
    scaling = 1.0 / math.sqrt(HEAD_DIM)
    query_heads = queries.reshape(req_here, drafts, groups, per_group, HEAD_DIM)
    cache_k = cache_keys.reshape(req_here, context_len, groups, HEAD_DIM)
    cache_v = cache_values.reshape(req_here, context_len, groups, HEAD_DIM)
    draft_k = draft_keys.reshape(req_here, drafts, groups, HEAD_DIM)
    draft_v = draft_values.reshape(req_here, drafts, groups, HEAD_DIM)
    score_cache = (
        jnp.einsum("rigpe,rcge->rgpic", query_heads, cache_k, preferred_element_type=jnp.float32)
        * scaling
    )
    score_draft = (
        jnp.einsum("rigpe,rjge->rgpij", query_heads, draft_k, preferred_element_type=jnp.float32)
        * scaling
    )
    live_cache = jnp.arange(context_len, dtype=jnp.int32)[None, :] < cache_lengths[:, None]
    live_draft = (
        jnp.arange(drafts, dtype=jnp.int32)[None, :] <= jnp.arange(drafts, dtype=jnp.int32)[:, None]
    )
    score_cache = jnp.where(live_cache[:, None, None, None, :], score_cache, -1e30)
    score_draft = jnp.where(live_draft[None, None, None, :, :], score_draft, -1e30)
    highest = jnp.maximum(jnp.max(score_cache, axis=-1), jnp.max(score_draft, axis=-1))
    expo_cache = jnp.exp(score_cache - highest[..., None])
    expo_draft = jnp.exp(score_draft - highest[..., None])
    totals = jnp.sum(expo_cache, axis=-1) + jnp.sum(expo_draft, axis=-1)
    prob_cache = (expo_cache / totals[..., None]).astype(jnp.bfloat16)
    prob_draft = (expo_draft / totals[..., None]).astype(jnp.bfloat16)
    result = jnp.einsum(
        "rgpic,rcge->rigpe", prob_cache, cache_v, preferred_element_type=jnp.float32
    )
    result = result + jnp.einsum(
        "rgpij,rjge->rigpe", prob_draft, draft_v, preferred_element_type=jnp.float32
    )
    return result.astype(jnp.bfloat16).reshape(req_here, drafts, query_width)


def ring(x, axis, k, n=4):
    k = k % n
    return x if k == 0 else lax.ppermute(x, axis, [(i, (i + k) % n) for i in range(n)])


def swap(x):
    return lax.ppermute(x, "core", [(0, 1), (1, 0)])


def after(x, *others):
    return lax.optimization_barrier((x, *others))[0]


def dot(a, b, dims, batch=()):
    return lax.dot_general(a, b, (dims, (batch, batch)), preferred_element_type=F32)


def split3(x):
    hi = lax.reduce_precision(x, 8, 7)
    mid = lax.reduce_precision(x - hi, 8, 7)
    lo = x - hi - mid
    return [v.astype(BF) for v in (hi, mid, lo)]


def settle_kernel(x_ref, *refs):
    pass


def settle(x, micros, *others):
    in_hbm = pl.BlockSpec(memory_space=pl.ANY)
    return pl.pallas_call(
        settle_kernel,
        out_shape=jax.ShapeDtypeStruct(x.shape, x.dtype),
        in_specs=[in_hbm] * (1 + len(others)),
        out_specs=in_hbm,
        input_output_aliases={0: 0},
        cost_estimate=pl.CostEstimate(
            flops=micros * 1_000_000_000, bytes_accessed=micros * 3_000_000, transcendentals=0
        ),
    )(x, *others)


def partial_kernel(x_ref, w_ref, out_ref):
    sources, lines, part = x_ref.shape
    per = w_ref.shape[0]
    chunk = lines // per
    x = x_ref[...].reshape(sources * lines, part)
    for s in range(per):
        y = jnp.dot(x, w_ref[s], preferred_element_type=F32).reshape(sources, lines, -1)
        y = y[:, s * chunk : (s + 1) * chunk].reshape(sources * chunk, -1)
        out_ref[pl.ds(s * sources * chunk, sources * chunk), :] = y.astype(out_ref.dtype)


def partial_sums(arrived, weights, dtype):
    sources, lines, part = arrived.shape
    return pl.pallas_call(
        partial_kernel,
        out_shape=jax.ShapeDtypeStruct((sources * lines, weights.shape[2]), dtype),
        compiler_params=pltpu.CompilerParams(vmem_limit_bytes=48 * 2**20),
        cost_estimate=pl.CostEstimate(
            flops=2 * sources * lines * part * weights.shape[2],
            bytes_accessed=2 * (arrived.size + weights.size),
            transcendentals=0,
        ),
    )(arrived, weights)


def place_kernel(picks, info_ref, hot_ref, plane_ref, rows_ref, out_ref, combine_ref, rank_ref):
    info = info_ref[...].astype(F32)
    tokens, slots = info.shape[0], hot_ref.shape[1]
    rows = tokens // 4
    chunk = out_ref.shape[0] // slots
    lane = lax.broadcasted_iota(jnp.int32, (tokens, slots), 1).astype(F32)
    takes = jnp.zeros((tokens, slots), F32)
    weights = [jnp.zeros((tokens, slots), F32) for _ in range(3)]
    for k in range(picks):
        match = lane == info[:, k : k + 1]
        takes = jnp.where(match, 1.0, takes)
        for i in range(3):
            at = (i + 1) * picks + k
            weights[i] = jnp.where(match, info[:, at : at + 1], weights[i])
    early = lax.broadcasted_iota(jnp.int32, (tokens, tokens), 1)
    late = lax.broadcasted_iota(jnp.int32, (tokens, tokens), 0)
    before = late > early
    for k in range(1, 4):
        before = before & ((late >= k * rows) == (early >= k * rows))
    rank = jnp.dot(
        before.astype(BF), takes.astype(BF), preferred_element_type=F32
    )
    rank_ref[...] = jnp.where(takes > 0, rank, -1.0)
    cold = (takes > 0) & (hot_ref[...] == 0)
    code = jnp.where(cold, plane_ref[...] * CAP + rank, -1.0)
    wide = slots * chunk
    slot_at = lax.broadcasted_iota(jnp.int32, (slots, wide), 0)
    column = lax.broadcasted_iota(jnp.int32, (slots, wide), 1)
    spread = (column // chunk == slot_at).astype(BF)
    code = jnp.dot(code.astype(BF), spread, preferred_element_type=F32)
    turn = lax.broadcasted_iota(jnp.int32, (tokens, wide), 1) % chunk
    place = code == turn.astype(F32)
    for i in range(3):
        spread_weight = jnp.dot(weights[i].astype(BF), spread, preferred_element_type=F32)
        combine_ref[i] = jnp.where(place, spread_weight, 0.0).astype(BF)
    out_ref[...] = lax.dot_general(
        place.astype(BF), rows_ref[...], (((0,), (0,)), ((), ())), preferred_element_type=F32
    ).astype(BF)


def place_rows(infos, hot, planes, my_part, picks, chunk):
    tokens, part = my_part.shape
    slots = hot.shape[1]
    return pl.pallas_call(
        functools.partial(place_kernel, picks),
        out_shape=(
            jax.ShapeDtypeStruct((slots * chunk, part), BF),
            jax.ShapeDtypeStruct((3, tokens, slots * chunk), BF),
            jax.ShapeDtypeStruct((tokens, slots), F32),
        ),
        compiler_params=pltpu.CompilerParams(vmem_limit_bytes=32 * 2**20),
        cost_estimate=pl.CostEstimate(
            flops=1_000_000_000, bytes_accessed=4_000_000, transcendentals=0
        ),
    )(infos, hot, planes, my_part)


def per_device(
    tokens,
    route_ids,
    route_weights,
    placement,
    gate_up,
    down,
    queries,
    draft_keys,
    draft_values,
    cache_keys,
    cache_values,
    cache_lengths,
):
    n_dp, n_x = lax.axis_size("dp"), lax.axis_size("x")
    n_expert = lax.axis_size(PLANE)
    me, here = lax.axis_index("dp"), lax.axis_index(PLANE)
    here_x, core = lax.axis_index("x"), lax.axis_index("core")
    rows, picks = route_ids.shape
    slots = placement.shape[0]
    per = gate_up.shape[0]
    width = tokens.shape[1]
    part = width // n_dp
    quarter = gate_up.shape[2] // 2
    chunk = n_dp * CAP
    all_rows = n_dp * rows
    slot_range = jnp.arange(slots, dtype=jnp.int32)
    ks, xs = range(n_dp), range(n_x)

    def plane(k):
        return (me + n_dp - k) % n_dp

    slot_of = jnp.sum(
        jnp.where(route_ids[:, :, None] == slot_range, placement, 0), axis=2
    )
    info = jnp.concatenate([slot_of.astype(BF)] + split3(route_weights), axis=1)
    info = jnp.pad(info, ((0, 0), (0, LANES - info.shape[1])))
    sent = jnp.concatenate([tokens, info], axis=1)
    came = [ring(sent, "dp", k) for k in ks]
    came_tokens = [x[:, :width] for x in came]
    infos = jnp.concatenate([x[:, width:] for x in came], axis=0)
    my_part = jnp.concatenate(
        [lax.dynamic_slice_in_dim(x, me * part, part, axis=1) for x in came_tokens], axis=0
    )

    own = jnp.sum(slot_of[:, :, None] == slot_range, axis=(0, 1))
    hot = own > CAP
    first_hot = jnp.min(jnp.where(hot, slot_range, slots - 1))
    last_hot = jnp.max(jnp.where(hot, slot_range, 0))
    my_hot = jnp.where(core == 0, first_hot, last_hot)
    other_hot = jnp.where(core == 0, last_hot, first_hot)

    owner = my_hot // per

    def on_owner(weights):
        theirs = swap(lax.dynamic_index_in_dim(weights, other_hot % per, 0, keepdims=False))
        mine = lax.dynamic_index_in_dim(weights, my_hot % per, 0, keepdims=False)
        return jnp.where(owner == here, mine, jnp.where(owner == here + 1 - 2 * core, theirs, 0.0))

    held = (on_owner(gate_up), on_owner(down))
    piece = lax.psum_scatter(held, "x", scatter_dimension=0, tiled=True)

    to_send = [
        lax.dynamic_slice_in_dim(gate_up, (me + k) % n_dp * part, part, axis=1) for k in ks
    ]
    pieces = [ring(x, "dp", k) for k, x in zip(ks, to_send)]

    plane_of = (me + n_dp - jnp.arange(all_rows, dtype=jnp.int32) // rows) % n_dp
    planes = plane_of.astype(F32)[:, None]
    my_part = settle(my_part, 20)
    my_part, *_ = lax.optimization_barrier((my_part, *held, *to_send))
    outgoing, combine, rank_of = place_rows(
        infos, hot[None, :].astype(jnp.int32), planes, my_part, picks, chunk
    )
    arrived = lax.all_to_all(
        outgoing.reshape(n_expert, per * chunk, part), PLANE, 0, 0, tiled=True
    )
    pieces[-1] = after(pieces[-1], *piece)

    pieces[2] = settle(pieces[2], 40)
    total = partial_sums(arrived, pieces[0], F32)
    for k in ks[1:]:
        total = total + ring(partial_sums(arrived, pieces[k], BF), "dp", -k).astype(F32)
    hidden = jax.nn.silu(total[:, :quarter]) * total[:, quarter:]
    hidden = jnp.swapaxes(hidden.astype(BF).reshape(per, -1, quarter), 1, 2)
    late = lax.optimization_barrier(
        (queries, draft_keys, draft_values, cache_keys, cache_values, cache_lengths, hidden)
    )
    context = attend_block(*late[:-1])
    outs = [0.0] * per
    for k in ks:
        hidden_k = ring(hidden, "dp", k)
        for s in range(per):
            down_piece = lax.dynamic_slice_in_dim(down[s], plane(k) * quarter, quarter, axis=0)
            outs[s] = outs[s] + dot(hidden_k[s], down_piece, ((0,), (0,)))
    out = jnp.concatenate([o.astype(BF).reshape(n_expert, chunk, part) for o in outs], axis=1)
    out = settle(out, 1, context)
    back = lax.all_to_all(out, PLANE, 0, 0, tiled=True).reshape(slots * chunk, part)

    came_slots = infos[:, :picks].astype(jnp.int32)
    came_weights = sum(infos[:, i * picks : (i + 1) * picks].astype(F32) for i in (1, 2, 3))

    def hot_rows_of(slot):
        rank = jnp.sum(jnp.where(slot_range == slot, rank_of, 0.0), axis=1).astype(jnp.int32)
        code = jnp.where(rank >= 0, plane_of * HOT_ROWS + rank, -1)
        find = code[None, :] == jnp.arange(n_dp * HOT_ROWS, dtype=jnp.int32)[:, None]
        weight = jnp.sum(jnp.where(came_slots == slot, came_weights, 0.0), axis=1)
        return find, jnp.where(find, weight, 0.0)

    came_all = jnp.concatenate(came_tokens, axis=0)
    find_mine, weigh_mine = hot_rows_of(my_hot)
    find_other, weigh_other = hot_rows_of(other_hot)
    half = n_dp * HOT_ROWS
    found = dot(jnp.concatenate([find_mine, find_other]).astype(BF), came_all, ((1,), (0,)))
    found = after(found.astype(BF), arrived)
    found = jnp.concatenate([found[:half], swap(found[half:])])

    def of_x(x, k, axis):
        size = x.shape[axis] // n_x
        return lax.dynamic_slice_in_dim(x, (here_x + k) % n_x * size, size, axis=axis)

    def back_to_x(x):
        size = x.shape[0] // n_x
        total = x[:size]
        for k in xs[1:]:
            sent_back = x[k * size : (k + 1) * size].astype(BF)
            total = total + ring(sent_back, "x", -k).astype(F32)
        return total

    x_rows = jnp.concatenate([ring(of_x(found, k, 1), "x", k) for k in xs])
    hot_gate, hot_down = lax.psum(piece, "z")
    hot_gate, hot_down, _ = lax.optimization_barrier((hot_gate, hot_down, out))
    gated = back_to_x(dot(x_rows, hot_gate, ((1,), (0,))))
    hidden_hot = (jax.nn.silu(gated[:, :quarter]) * gated[:, quarter:]).astype(BF)
    hidden_all = jnp.zeros((n_dp * 2 * half, quarter), BF)
    for k in ks:
        hidden_all = lax.dynamic_update_slice_in_dim(
            hidden_all, ring(hidden_hot, "dp", k), plane(k) * 2 * half, axis=0
        )
    x_hidden = jnp.concatenate([ring(of_x(hidden_all, k, 0), "x", k) for k in xs])
    hot_out = back_to_x(dot(x_hidden, hot_down, ((1,), (0,)))).astype(BF)
    hot_outs = jnp.concatenate([hot_out[:half], swap(hot_out[half:])])
    weigh = jnp.concatenate([weigh_mine, weigh_other])

    mixed = dot(combine[0], back, ((1,), (0,)))
    for i in (1, 2):
        mixed = mixed + dot(combine[i], back, ((1,), (0,)))
    for weigh_i in split3(weigh):
        mixed = mixed + dot(weigh_i, hot_outs, ((0,), (0,)))

    mixed = mixed.astype(BF).reshape(n_dp, rows, part)
    mixed_out = jnp.zeros((rows, width), BF)
    for k in ks:
        mixed_out = lax.dynamic_update_slice_in_dim(
            mixed_out, ring(mixed[k], "dp", -k), (me + k) % n_dp * part, axis=1
        )
    return (mixed_out, context)


def solution(mesh):
    chips = Mesh(mesh.devices.reshape(mesh.shape["dp"], 4, -1, 2), ALL)
    in_specs = (
        P(ALL, None),
        P(ALL, None),
        P(ALL, None),
        P(),
        P(PLANE, None, "dp"),
        P(PLANE, None, "dp"),
        P(ALL, None, None),
        P(ALL, None, None),
        P(ALL, None, None),
        P(ALL, None, None),
        P(ALL, None, None),
        P(ALL),
    )
    out_specs = (P(ALL, None), P(ALL, None, None))
    return jax.shard_map(
        per_device, mesh=chips, in_specs=in_specs, out_specs=out_specs, check_vma=False
    )
```
